512 devices in a mesh: group: 16 (over y, z_hi), tile: 32 (over z_lo, x, core).
Axes of the slice: x: 4, y: 4, z: 16 (z_hi: 4, z_lo: 4; z = z_hi * 4 + z_lo), core: 2. Of those that a mesh axis runs over, the one named last changes fastest.
Arguments:
- features: bfloat16 [1024, 512, 128], P(('group', 'tile')), may hold values from -6 to 6
- occupancy: int32 [1024, 512], P(('group', 'tile')), may hold values 0 or 1
- block_pos: int32 [1024], P(('group', 'tile')), may hold values from -1 to 7, as said below
- kernel: bfloat16 [27, 128, 128], replicated, may hold values from -0.109375 to 0.109375
- out_grad: bfloat16 [1024, 512, 128], P(('group', 'tile')), may hold values from -6 to 6
Outputs:
- conv_out: bfloat16 [1024, 512, 128], P(('group', 'tile'))
- feature_grad: bfloat16 [1024, 512, 128], P(('group', 'tile'))
- kernel_grad: float32 [27, 128, 128], replicated
The draws below stay inside these ranges and needn't reach their ends.
Inputs may be any that keep to these rules, and one draw needn't show every extreme that they name: `block_pos`: within each device's 2 slots the filled ones come first and hold distinct block heights; -1 marks an empty slot. Every device fills at least one slot and some device fills all 2.
All inputs are finite; a program needn't handle non-finite values. No bound on the sum of `occupancy` on one device may be relied on, other than what follows from the above.
Results may differ from the reference program's by a relative error of at most 0.001.
Values may be sent and summed in bfloat16 or wider, within the bound.
No kernel may reach another device: no remote copies, remote signals or barrier semaphores. Data moves between devices by JAX's collectives and lax.ppermute only.
A program may use at most 128 MiB of HBM per device.

```python
import math
import jax
import jax.numpy as jnp
from jax import lax

BE = 8
VOX = 512
C = 128
KV = 27
BLK_DEV = 2
GZ = 8
BLOCKS = 1024
N_GROUP = 16
N_TILE = 32


def draw_block_pos(key, part):
    key = jax.random.fold_in(key, 11)
    key_rank, key_count, key_full = jax.random.split(key, 3)
    devices = BLOCKS // BLK_DEV
    device_ids = jnp.arange(devices, dtype=jnp.int32)
    heights = jnp.arange(GZ, dtype=jnp.int32)
    ranking = jax.random.randint(key_rank, (devices, GZ), 0, 1 << 20) * GZ + heights[None, :]
    full_device = jax.random.randint(key_full, (), 0, devices)
    ranking = jnp.where((device_ids[:, None] == full_device) & (heights[None, :] == GZ - 1), -1, ranking)
    chosen = jnp.argsort(ranking, axis=1)[:, :BLK_DEV].astype(jnp.int32)
    counts = jax.random.randint(key_count, (devices,), 1, BLK_DEV + 1)
    counts = jnp.where(device_ids == full_device, BLK_DEV, counts)
    counts = jnp.where(device_ids == (full_device + 1) % devices, 1, counts)
    slot_index = jnp.arange(BLK_DEV, dtype=jnp.int32)
    positions = jnp.where(slot_index[None, :] < counts[:, None], chosen, -1)
    return positions.reshape(BLOCKS).astype(jnp.int32)


def with_ends(array, key, smallest, top_value):
    longest = array.shape.index(max(array.shape))
    spots = []
    for shift in (0, 1):
        where = [jax.random.randint(jax.random.fold_in(key, axis), (), 0, length) for axis, length in enumerate(array.shape)]
        where[longest] = (where[longest] + shift) % array.shape[longest]
        spots.append(tuple(where))
    return array.at[spots[0]].set(smallest).at[spots[1]].set(top_value)


def block_scale(rng, extent, shards, low, high):
    factor_of, own = 1.0, jax.random.fold_in(rng, 6)
    for dim, parts in shards:
        steps = jnp.exp(jax.random.uniform(jax.random.fold_in(own, dim), (parts,), jnp.float32, low / len(shards), high / len(shards)))
        factor_of = factor_of * jnp.repeat(steps, extent[dim] // parts).reshape([-1 if axis == dim else 1 for axis in range(len(extent))])
    return factor_of


def gaussian(stream_key, dims, deviation, bound, cuts=(), held_as=jnp.bfloat16):
    loudness = block_scale(stream_key, dims, cuts, -0.22, 0.18) if cuts else 1.0
    result = jax.random.normal(stream_key, dims, jnp.float32) * deviation * loudness
    return jnp.minimum(jnp.maximum(result, -bound), bound).astype(held_as)


def setup_inputs(seed: int = 0) -> dict:
    key_list = jax.random.split(jax.random.key(seed), 6)
    return {
        "features": gaussian(key_list[0], (BLOCKS, VOX, C), 1.0, 6.0, ((0, 512),)),
        "occupancy": with_ends((jax.random.randint(key_list[1], (BLOCKS, VOX), 0, 4) < 3).astype(jnp.int32), jax.random.fold_in(key_list[1], 1), 0, 1),
        "block_pos": draw_block_pos(jax.random.fold_in(key_list[5], 71), 0),
        "kernel": gaussian(key_list[3], (KV, C, C), (KV * C) ** -0.5, 0.109375),
        "out_grad": gaussian(key_list[4], (BLOCKS, VOX, C), 1.0, 6.0, ((0, 512),)),
    }


def build_column(block_field, positions):
    heights = jnp.arange(GZ, dtype=jnp.int32)
    onehot = (heights[:, None] == positions[None, :]).astype(jnp.float32)
    blocks = block_field.astype(jnp.float32).reshape(BLK_DEV, BE, BE, BE, C)
    placed = jnp.einsum('zs,sxyvc->xyzvc', onehot, blocks)
    return placed.reshape(BE, BE, GZ * BE, C).astype(jnp.bfloat16)

def slot_stack(padded, position):
    lower_z = (BE * jnp.maximum(position, 0)).astype(jnp.int32)
    anchor_index = jnp.zeros((), jnp.int32)
    window = lax.dynamic_slice(padded, (anchor_index, anchor_index, lower_z, anchor_index), (BE + 2, BE + 2, BE + 2, C))
    pieces = [window[step_x:step_x + BE, step_y:step_y + BE, step_z:step_z + BE].reshape(VOX, C) for step_x in range(3) for step_y in range(3) for step_z in range(3)]
    return jnp.stack(pieces)

def reference(features, occupancy, block_pos, kernel, out_grad):
    slot_live = (block_pos >= 0).astype(jnp.float32)
    active = occupancy.astype(jnp.float32) * slot_live[:, None]
    masked_in = (features.astype(jnp.float32) * active[:, :, None]).astype(jnp.bfloat16)
    masked_grad = (out_grad.astype(jnp.float32) * active[:, :, None]).astype(jnp.bfloat16)
    grid_shape = (N_GROUP, N_TILE, BLK_DEV, VOX, C)
    in_grid = masked_in.reshape(grid_shape)
    grad_grid = masked_grad.reshape(grid_shape)
    positions = block_pos.reshape(N_GROUP, N_TILE, BLK_DEV)
    active_grid = active.reshape(N_GROUP, N_TILE, BLK_DEV, VOX)
    kernel_float = kernel.astype(jnp.float32)
    kernel_flipped = kernel_float[::-1]

    def neighbourhood(grid, group_index):
        near_groups = group_index + jnp.arange(3, dtype=jnp.int32) - 1
        inside = (near_groups >= 0) & (near_groups < N_GROUP)
        clipped = jnp.clip(near_groups, 0, N_GROUP - 1).astype(jnp.int32)
        chosen = jnp.where(inside[:, None, None, None, None], grid[clipped], jnp.zeros((), jnp.bfloat16))
        heights = positions[clipped]
        columns = jax.vmap(jax.vmap(build_column))(chosen, heights)
        columns = jnp.pad(columns, ((0, 0), (1, 1), (0, 0), (0, 0), (0, 0), (0, 0)))

        def one_tile(tile_index):
            nearby = lax.dynamic_slice_in_dim(columns, tile_index, 3, 1)
            joined = nearby.transpose(0, 2, 1, 3, 4, 5).reshape(3 * BE, 3 * BE, GZ * BE, C)
            trimmed = joined[BE - 1:2 * BE + 1, BE - 1:2 * BE + 1]
            return jnp.pad(trimmed, ((0, 0), (0, 0), (1, 1), (0, 0)))
        return jax.vmap(one_tile)(jnp.arange(N_TILE, dtype=jnp.int32))
    stack_slots = jax.vmap(jax.vmap(slot_stack, in_axes=(None, 0)), in_axes=(0, 0))

    def per_group(group_index):
        padded_in = neighbourhood(in_grid, group_index)
        padded_grad = neighbourhood(grad_grid, group_index)
        heights = positions[group_index]
        stack_in = stack_slots(padded_in, heights).astype(jnp.float32)
        stack_grad = stack_slots(padded_grad, heights).astype(jnp.float32)
        slot_masks = active_grid[group_index][..., None]
        conv_block = jnp.einsum('tskvc,kcd->tsvd', stack_in, kernel_float) * slot_masks
        back_block = jnp.einsum('tskvd,kcd->tsvc', stack_grad, kernel_flipped) * slot_masks
        own_grad = grad_grid[group_index].astype(jnp.float32)
        group_part = jnp.einsum('tskvc,tsvd->kcd', stack_in, own_grad)
        return (conv_block.astype(jnp.bfloat16), back_block.astype(jnp.bfloat16), group_part)
    conv_all, back_all, group_parts = lax.map(per_group, jnp.arange(N_GROUP, dtype=jnp.int32))
    kernel_grad = lax.optimization_barrier(jnp.sum(group_parts, axis=0)) / math.sqrt(BLOCKS * VOX)
    return (conv_all.reshape(BLOCKS, VOX, C), back_all.reshape(BLOCKS, VOX, C), kernel_grad)
```

```python
import math

import jax
import jax.numpy as jnp
from jax import lax
from jax.experimental import pallas as pl
from jax.experimental.pallas import tpu as pltpu
from jax.sharding import PartitionSpec as P

BE = 8
VOX = 512
C = 128
KV = 27
BLK_DEV = 2
WIN = BE + 2
SLAB = WIN * BE * BE
SIDE = 9 * C
AXES = ("group", "tile")
FACE = 2 * BLK_DEV * BE * BE
EDGE = 2 * BLK_DEV * BE
TAG = 16
CHUNK = 112
HALF = 16 * CHUNK
CORE = 1
X_SETS = [[z * 8 + x * 2 + core for x in range(4)] for z in range(4) for core in range(2)]
Z_LO_SETS = [[z * 8 + x * 2 + core for z in range(4)] for x in range(4) for core in range(2)]
Y_SETS = [[y * 4 + z for y in range(4)] for z in range(4)]
Z_HI_BITS = (32, 96)


def tags(pos_ref):
    return jnp.concatenate(
        [jnp.full((BE, C), pos_ref[s].astype(jnp.float32), jnp.float32) for s in range(BLK_DEV)]
    ).astype(jnp.bfloat16)


def prep_kernel(pos_ref, occ_ref, feat_ref, grad_ref, in_ref, g_ref, mask_ref, ylo_ref, yhi_ref):
    occ = occ_ref[...].astype(jnp.float32)
    for face in (ylo_ref, yhi_ref):
        face[FACE:FACE + TAG, :] = tags(pos_ref)
    for s in range(BLK_DEV):
        live = (pos_ref[s] >= 0).astype(jnp.float32)
        mask = jnp.concatenate([
            jnp.broadcast_to(occ[s:s + 1, r * C:(r + 1) * C] * live, (C, C)).T for r in range(VOX // C)
        ])
        mask_ref[s * VOX:(s + 1) * VOX, :] = mask.astype(jnp.bfloat16)
        for field, (src, dst) in enumerate(((feat_ref, in_ref), (grad_ref, g_ref))):
            value = jnp.where(mask > 0, src[s].astype(jnp.float32), 0.0)
            dst[s * VOX:(s + 1) * VOX, :] = value.astype(jnp.bfloat16)
            cube = value.reshape(BE, BE, BE, C)
            at = (field * BLK_DEV + s) * BE * BE
            here = slice(at, at + BE * BE)
            ylo_ref[here, :] = cube[:, 0].reshape(BE * BE, C).astype(jnp.bfloat16)
            yhi_ref[here, :] = cube[:, BE - 1].reshape(BE * BE, C).astype(jnp.bfloat16)


def x_faces_kernel(pos_ref, in_ref, g_ref, low_ref, high_ref, xlo_ref, xhi_ref):
    for x, out in ((0, xlo_ref), (BE - 1, xhi_ref)):
        for field, own in enumerate((in_ref, g_ref)):
            for s in range(BLK_DEV):
                at = (field * BLK_DEV + s) * BE * BE
                first = s * VOX + x * BE * BE
                out[at:at + BE * BE, :] = own[first:first + BE * BE, :]
        for side, ref in enumerate((low_ref, high_ref)):
            edge = [
                ref[n * BE * BE:(n + 1) * BE * BE, :].astype(jnp.float32)[x * BE:(x + 1) * BE]
                for n in range(2 * BLK_DEV)
            ]
            at = FACE + side * EDGE
            out[at:at + EDGE, :] = jnp.concatenate(edge).astype(jnp.bfloat16)
            at = FACE + 2 * EDGE + side * TAG
            out[at:at + TAG, :] = ref[FACE:FACE + TAG, :]
        at = FACE + 2 * EDGE + 2 * TAG
        out[at:at + TAG, :] = tags(pos_ref)


def fill_windows(field, slots, pos_ref, own_ref, y_from, x_from, z_ref, a_ref):
    row = lax.broadcasted_iota(jnp.int32, (BE, C), 0)
    first = field * BLK_DEV
    regions = []

    def face_of(ref, shape):
        return [
            ref[n * BE * BE:(n + 1) * BE * BE, :].astype(jnp.float32).reshape(shape)
            for n in range(first, first + BLK_DEV)
        ]

    def tags_of(ref, at):
        tag = ref[at:at + TAG, :].astype(jnp.float32)
        return [tag[0:BE], tag[BE:2 * BE]]

    own = [own_ref[n * VOX:(n + 1) * VOX, :].astype(jnp.float32).reshape(BE, BE, BE, C) for n in range(BLK_DEV)]
    own_tags = [jnp.full((BE, C), pos_ref[n].astype(jnp.float32), jnp.float32) for n in range(BLK_DEV)]
    inside = slice(1, BE + 1)
    ends = (slice(0, 1), slice(WIN - 1, WIN))
    regions.append((inside, inside, own, own_tags))
    for ref, end in zip(y_from, ends):
        regions.append((inside, end, face_of(ref, (BE, 1, BE, C)), tags_of(ref, FACE)))
    for ref, end in zip(x_from, ends):
        regions.append((end, inside, face_of(ref, (1, BE, BE, C)), tags_of(ref, FACE + 2 * EDGE + 2 * TAG)))
        for side, other in enumerate(ends):
            edge = ref[FACE + side * EDGE:FACE + (side + 1) * EDGE, :].astype(jnp.float32)
            data = [edge[n * BE:(n + 1) * BE].reshape(1, 1, BE, C) for n in range(first, first + BLK_DEV)]
            regions.append((end, other, data, tags_of(ref, FACE + 2 * EDGE + side * TAG)))

    for i, s in enumerate(slots):
        here = pos_ref[s].astype(jnp.float32)
        for xs, ys, data, tags in regions:
            delta = [tag - here for tag in tags]
            for o3 in range(3):
                picks = []
                for n in range(BLK_DEV):
                    if o3 == 0:
                        wanted = jnp.where(row == 0, -1.0, 0.0)
                        moved = pltpu.roll(data[n].reshape(-1, BE, C), 1, 1)
                    elif o3 == 2:
                        wanted = jnp.where(row == BE - 1, 1.0, 0.0)
                        moved = pltpu.roll(data[n].reshape(-1, BE, C), BE - 1, 1)
                    else:
                        wanted = jnp.zeros((BE, C), jnp.float32)
                        moved = data[n].reshape(-1, BE, C)
                    picks.append(((delta[n] == wanted)[None], moved))
                value = jnp.where(picks[1][0], picks[1][1], 0.0)
                value = jnp.where(picks[0][0], picks[0][1], value)
                z_ref[o3, xs, ys] = value.reshape(data[0].shape)
        for o2 in range(3):
            for o3 in range(3):
                j = o2 * 3 + o3
                piece = z_ref[o3, :, o2:o2 + BE].reshape(SLAB, C)
                a_ref[i, :, j * C:(j + 1) * C] = piece.astype(jnp.bfloat16)


def wgrad_kernel(scale, pos_ref, core_ref, in_ref, g_ref, *refs):
    halo, keep_ref, send_ref, z_ref, a_ref, total_ref = refs[:4], *refs[-5:]
    fill_windows(1, (0, 1), pos_ref, g_ref, halo[0:2], halo[2:4], z_ref, a_ref)
    inner = [
        jnp.transpose(in_ref[s * VOX:(s + 1) * VOX, :].astype(jnp.float32)).astype(jnp.bfloat16)
        for s in range(BLK_DEV)
    ]
    total_ref[KV * C:, :] = jnp.zeros((2 * HALF - KV * C, C), jnp.float32)
    for e1 in range(3):
        rows = slice(e1 * BE * BE, e1 * BE * BE + VOX)
        total = jnp.dot(inner[0], a_ref[0, rows, :], preferred_element_type=jnp.float32)
        total = total + jnp.dot(inner[1], a_ref[1, rows, :], preferred_element_type=jnp.float32)
        total = total * scale
        for j in range(9):
            k = KV - 1 - (9 * e1 + j)
            total_ref[k * C:(k + 1) * C, :] = total[:, j * C:(j + 1) * C]
    core = core_ref[0]
    keep_ref[...] = total_ref[pl.ds(pl.multiple_of(core * HALF, HALF), HALF), :]
    send_ref[...] = total_ref[pl.ds(pl.multiple_of((1 - core) * HALF, HALF), HALF), :]


def place_kernel(core_ref, near_ref, far_ref, out_ref):
    first = core_ref[0] == 0
    rest = KV * C - HALF
    out_ref[0:HALF, :] = jnp.where(first, near_ref[...], far_ref[...])
    out_ref[HALF:KV * C, :] = jnp.where(first, far_ref[0:rest, :], near_ref[0:rest, :])


def turn_kernel(w_ref, out_ref, done_ref):
    for k in range(KV):
        at = (KV - 1 - k) * C
        out_ref[at:at + C, :] = jnp.transpose(w_ref[k * C:(k + 1) * C, :].astype(jnp.float32)).astype(jnp.bfloat16)
    done_ref[...] = jnp.zeros_like(done_ref)


def conv_kernel(field, slot, pos_ref, own_ref, mask_ref, w_ref, *refs):
    halo, out_ref, done_ref, z_ref, a_ref = refs[:4], *refs[-4:]
    fill_windows(field, (slot,), pos_ref, own_ref, halo[0:2], halo[2:4], z_ref, a_ref)
    total = None
    for e1 in range(3):
        rows = slice(e1 * BE * BE, e1 * BE * BE + VOX)
        part = jnp.dot(
            a_ref[0, rows, :], w_ref[e1 * SIDE:(e1 + 1) * SIDE, :], preferred_element_type=jnp.float32
        )
        total = part if total is None else total + part
    mask = mask_ref[slot * VOX:(slot + 1) * VOX, :].astype(jnp.float32)
    out_ref[0] = jnp.where(mask > 0, total, 0.0).astype(jnp.bfloat16)
    done_ref[...] = jnp.zeros_like(done_ref)


VMEM = pl.BlockSpec(memory_space=pltpu.VMEM)
ANY = pl.BlockSpec(memory_space=pl.ANY)
SMEM = pl.BlockSpec(memory_space=pltpu.SMEM)
PARAMS = pltpu.CompilerParams(vmem_limit_bytes=40 * 1024 * 1024)


def bf16(*shape):
    return jax.ShapeDtypeStruct(shape, jnp.bfloat16)


def whole(*shape):
    return pl.BlockSpec(shape, lambda i: (0,) * len(shape))


def prep(block_pos, occupancy, features, out_grad):
    return pl.pallas_call(
        prep_kernel,
        grid=(1,),
        out_shape=[bf16(BLK_DEV * VOX, C)] * 3 + [bf16(FACE + TAG, C)] * 2,
        in_specs=[SMEM, whole(BLK_DEV, VOX)] + [whole(BLK_DEV, VOX, C)] * 2,
        out_specs=[VMEM] * 5,
        compiler_params=PARAMS,
        name="mask_and_faces",
    )(block_pos, occupancy, features, out_grad)


def x_faces(block_pos, own_in, own_grad, low, high):
    return pl.pallas_call(
        x_faces_kernel,
        out_shape=[bf16(FACE + 2 * EDGE + 3 * TAG, C)] * 2,
        in_specs=[SMEM] + [VMEM] * 4,
        out_specs=[VMEM] * 2,
        compiler_params=PARAMS,
        name="x_faces",
    )(block_pos, own_in, own_grad, low, high)


def turn(weights, after):
    def kernel(w_ref, after_ref, *refs):
        turn_kernel(w_ref, *refs)

    return pl.pallas_call(
        kernel,
        out_shape=[bf16(KV * C, C), jax.ShapeDtypeStruct((BE, C), jnp.float32)],
        in_specs=[VMEM, ANY],
        out_specs=[VMEM] * 2,
        compiler_params=PARAMS,
        name="turn_weights",
    )(weights, after)


def scratch(slots):
    return [
        pltpu.VMEM((3, WIN, WIN, BE, C), jnp.float32),
        pltpu.VMEM((slots, SLAB, SIDE), jnp.bfloat16),
    ]


def wgrad(scale, block_pos, core, own_in, own_grad, halo, after):
    def kernel(*refs):
        wgrad_kernel(scale, *refs)

    half = jax.ShapeDtypeStruct((HALF, C), jnp.float32)
    return pl.pallas_call(
        kernel,
        out_shape=[half, half],
        in_specs=[SMEM] * 2 + [VMEM] * 6 + [ANY],
        out_specs=[VMEM] * 2,
        scratch_shapes=scratch(BLK_DEV) + [pltpu.VMEM((2 * HALF, C), jnp.float32)],
        compiler_params=PARAMS,
        name="kernel_gradient",
    )(block_pos, core, own_in, own_grad, *halo, after)


def place(core, near, far):
    return pl.pallas_call(
        place_kernel,
        out_shape=jax.ShapeDtypeStruct((KV * C, C), jnp.float32),
        in_specs=[SMEM] + [VMEM] * 2,
        out_specs=VMEM,
        compiler_params=PARAMS,
        name="place_halves",
    )(core, near, far)


def conv(field, slot, block_pos, own, mask, weights, halo, before, after):
    def kernel(*refs):
        conv_kernel(field, slot, *refs)

    flops = 2 * KV * VOX * C * C
    args = (block_pos, own, mask, weights, *halo)
    extra = ([] if before is None else [before]) + list(after)
    return pl.pallas_call(
        kernel,
        grid=(1,),
        out_shape=[bf16(BLK_DEV, VOX, C), jax.ShapeDtypeStruct((BE, C), jnp.float32)],
        in_specs=[SMEM] + [VMEM] * (len(args) - 1) + [ANY] * len(extra),
        out_specs=[pl.BlockSpec((1, VOX, C), lambda i: (slot, 0, 0)), VMEM],
        scratch_shapes=scratch(1),
        input_output_aliases={} if before is None else {len(args): 0},
        compiler_params=PARAMS,
        cost_estimate=pl.CostEstimate(flops=4 * flops, bytes_accessed=2_000_000, transcendentals=0),
        name=("convolution", "feature_gradient")[field],
    )(*args, *extra)


def small(kernel, outs, args, after=()):
    after = [v for v in after if v is not None]

    def inner(*refs):
        kernel(*refs[:len(args)], *refs[len(args) + len(after):])

    many = [jax.ShapeDtypeStruct((rows, C), jnp.float32) for rows in outs]
    return pl.pallas_call(
        inner,
        out_shape=many,
        in_specs=[VMEM] * len(args) + [ANY] * len(after),
        out_specs=[VMEM] * len(many),
        compiler_params=PARAMS,
        name=kernel.__name__.removesuffix("_kernel"),
    )(*args, *after)


def sum_two_kernel(a_ref, b_ref, out_ref):
    size = a_ref.shape[0]
    total = a_ref[...] + b_ref[...]
    for copy in range(out_ref.shape[0] // size):
        out_ref[copy * size:(copy + 1) * size, :] = total


def copies_kernel(a_ref, out_ref):
    size = a_ref.shape[0]
    for copy in range(out_ref.shape[0] // size):
        out_ref[copy * size:(copy + 1) * size, :] = a_ref[...]


def sum_four_kernel(a_ref, out_ref):
    size = a_ref.shape[0] // 4
    b = [a_ref[s * size:(s + 1) * size, :] for s in range(4)]
    total = (b[0] + b[1]) + (b[2] + b[3])
    for copy in range(out_ref.shape[0] // size):
        out_ref[copy * size:(copy + 1) * size, :] = total


def shifted(value, groups, tiles, up_g, up_t):
    pairs = [
        (g * tiles + t, (g + up_g) * tiles + t + up_t)
        for g in range(groups)
        for t in range(tiles)
        if 0 <= g + up_g < groups and 0 <= t + up_t < tiles
    ]
    return lax.ppermute(value, AXES, pairs)


def across(value, mask):
    count = lax.axis_size("group") * lax.axis_size("tile")
    return lax.ppermute(value, AXES, [(i, i ^ mask) for i in range(count)])


def exchange(value, axis, sets):
    rows = value.shape[0] // 4
    blocks = lax.all_to_all(value.reshape(4, rows, C), axis, 0, 0, axis_index_groups=sets)
    return blocks.reshape(4 * rows, C)


def body(features, occupancy, block_pos, kernel, out_grad):
    groups, tiles = lax.axis_size("group"), lax.axis_size("tile")
    core = (lax.axis_index("tile") & 1).astype(jnp.int32).reshape(1)
    own_in, own_grad, mask, ylo, yhi = prep(block_pos, occupancy, features, out_grad)
    y_from = (shifted(yhi, groups, tiles, 0, 1), shifted(ylo, groups, tiles, 0, -1))
    xlo, xhi = x_faces(block_pos, own_in, own_grad, *y_from)
    x_from = (shifted(xhi, groups, tiles, 1, 0), shifted(xlo, groups, tiles, -1, 0))
    halo = (*y_from, *x_from)
    weights = kernel.reshape(KV * C, C)
    turned, done = turn(weights, xhi)
    scale = 1.0 / math.sqrt(groups * tiles * BLK_DEV * VOX)
    keep, send = wgrad(scale, block_pos, core, own_in, own_grad, halo, done)

    def convolved(field, slot, before, *after):
        return conv(
            field, slot, block_pos, (own_in, own_grad)[field], mask, (weights, turned)[field],
            halo, before, after,
        )

    got = across(send, CORE)
    conv_out, done = convolved(0, 0, None, send)
    value, = small(sum_two_kernel, [HALF], [keep, got], [done])
    value, = small(sum_four_kernel, [4 * CHUNK], [exchange(value, "tile", X_SETS)])
    value, = small(sum_four_kernel, [4 * CHUNK], [exchange(value, "group", Y_SETS)])
    value, = small(sum_four_kernel, [CHUNK], [exchange(value, "tile", Z_LO_SETS)])
    got = across(value, Z_HI_BITS[0])
    conv_out, done = convolved(0, 1, conv_out, value)
    value, = small(sum_two_kernel, [CHUNK], [value, got], [done])
    got = across(value, Z_HI_BITS[1])
    feature_grad, done = convolved(1, 0, None, value)
    value, = small(sum_two_kernel, [4 * CHUNK], [value, got], [done])
    value = exchange(value, "group", Y_SETS)
    value, = small(copies_kernel, [HALF], [value])
    value = exchange(value, "tile", X_SETS)
    got = across(value, CORE)
    feature_grad, done = convolved(1, 1, feature_grad, value)
    total = place(core, value, got)
    return (conv_out, feature_grad, total.reshape(KV, C, C))


def solution(mesh):
    in_specs = (
        P(AXES, None, None),
        P(AXES, None),
        P(AXES),
        P(),
        P(AXES, None, None),
    )
    out_specs = (P(AXES, None, None), P(AXES, None, None), P())
    return jax.shard_map(body, mesh=mesh, in_specs=in_specs, out_specs=out_specs, check_vma=False)
```

```python
import math

import jax
import jax.numpy as jnp
from jax import lax
from jax.experimental import pallas as pl
from jax.experimental.pallas import tpu as pltpu
from jax.sharding import PartitionSpec as P

BE = 8
VOX = 512
C = 128
KV = 27
BLK_DEV = 2
WIN = BE + 2
SLAB = WIN * BE * BE
SIDE = 9 * C
AXES = ("group", "tile")
FACE = 2 * BLK_DEV * BE * BE
EDGE = 2 * BLK_DEV * BE
TAG = 16
CHUNK = 112
CODED = CHUNK + TAG
STEPS = 32000.0
HALF = 16 * CHUNK
CORE = 1
XY_SETS = [
    [(y * 4 + z_hi) * 32 + z_lo * 8 + x * 2 + core for y in range(4) for x in range(4)]
    for z_hi in range(4) for z_lo in range(4) for core in range(2)
]
Z_LO_SETS = [[z * 8 + x * 2 + core for z in range(4)] for x in range(4) for core in range(2)]
Z_HI_BITS = (32, 96)


def tags(pos_ref):
    return jnp.concatenate(
        [jnp.full((BE, C), pos_ref[s].astype(jnp.float32), jnp.float32) for s in range(BLK_DEV)]
    ).astype(jnp.bfloat16)


def prep_kernel(*refs):
    sources, (in_ref, g_ref, mask_ref, xlo_ref, xhi_ref), held, sems = refs[:4], refs[4:9], refs[9:13], refs[13]
    copies = [pltpu.make_async_copy(src, dst, sems.at[i]) for i, (src, dst) in enumerate(zip(sources, held))]
    for copy in copies:
        copy.start()
    for copy in copies:
        copy.wait()
    pos_ref, occ_ref, feat_ref, grad_ref = held
    occ = occ_ref[...].astype(jnp.float32)
    layer = BE * BE
    for face in (xlo_ref, xhi_ref):
        face[FACE:FACE + TAG, :] = tags(pos_ref)
    for s in range(BLK_DEV):
        live = (pos_ref[s] >= 0).astype(jnp.float32)
        mask = jnp.concatenate([
            jnp.broadcast_to(occ[s:s + 1, r * C:(r + 1) * C] * live, (C, C)).T for r in range(VOX // C)
        ])
        mask_ref[s * VOX:(s + 1) * VOX, :] = mask.astype(jnp.bfloat16)
        for field, (src, dst) in enumerate(((feat_ref, in_ref), (grad_ref, g_ref))):
            value = jnp.where(mask > 0, src[s].astype(jnp.float32), 0.0).astype(jnp.bfloat16)
            dst[s * VOX:(s + 1) * VOX, :] = value
            at = (field * BLK_DEV + s) * layer
            xlo_ref[at:at + layer, :] = value[:layer]
            xhi_ref[at:at + layer, :] = value[VOX - layer:]


def y_faces_kernel(pos_ref, in_ref, g_ref, low_ref, high_ref, ylo_ref, yhi_ref):
    layer = BE * BE
    for field, own in enumerate((in_ref, g_ref)):
        for s in range(BLK_DEV):
            cube = own[s * VOX:(s + 1) * VOX, :].astype(jnp.float32).reshape(BE, BE, BE, C)
            at = (field * BLK_DEV + s) * layer
            for y, out in ((0, ylo_ref), (BE - 1, yhi_ref)):
                out[at:at + layer, :] = cube[:, y].reshape(layer, C).astype(jnp.bfloat16)
    for side, ref in enumerate((low_ref, high_ref)):
        faces = [ref[n * layer:(n + 1) * layer, :].astype(jnp.float32) for n in range(2 * BLK_DEV)]
        for y, out in ((0, ylo_ref), (BE - 1, yhi_ref)):
            edge = [face[y * BE:(y + 1) * BE] for face in faces]
            at = FACE + side * EDGE
            out[at:at + EDGE, :] = jnp.concatenate(edge).astype(jnp.bfloat16)
            at = FACE + 2 * EDGE + side * TAG
            out[at:at + TAG, :] = ref[FACE:FACE + TAG, :]
    at = FACE + 2 * EDGE + 2 * TAG
    for out in (ylo_ref, yhi_ref):
        out[at:at + TAG, :] = tags(pos_ref)


def fill_windows(field, slots, pos_ref, own_ref, x_from, y_from, z_ref, a_ref):
    row = lax.broadcasted_iota(jnp.int32, (BE, C), 0)
    first = field * BLK_DEV
    regions = []

    def face_of(ref, shape):
        return [
            ref[n * BE * BE:(n + 1) * BE * BE, :].astype(jnp.float32).reshape(shape)
            for n in range(first, first + BLK_DEV)
        ]

    def tags_of(ref, at):
        tag = ref[at:at + TAG, :].astype(jnp.float32)
        return [tag[0:BE], tag[BE:2 * BE]]

    own = [own_ref[n * VOX:(n + 1) * VOX, :].astype(jnp.float32).reshape(BE, BE, BE, C) for n in range(BLK_DEV)]
    own_tags = [jnp.full((BE, C), pos_ref[n].astype(jnp.float32), jnp.float32) for n in range(BLK_DEV)]
    inside = slice(1, BE + 1)
    ends = (slice(0, 1), slice(WIN - 1, WIN))
    regions.append((inside, inside, own, own_tags))
    for ref, end in zip(x_from, ends):
        regions.append((end, inside, face_of(ref, (1, BE, BE, C)), tags_of(ref, FACE)))
    for ref, end in zip(y_from, ends):
        regions.append((inside, end, face_of(ref, (BE, 1, BE, C)), tags_of(ref, FACE + 2 * EDGE + 2 * TAG)))
        for side, other in enumerate(ends):
            edge = ref[FACE + side * EDGE:FACE + (side + 1) * EDGE, :].astype(jnp.float32)
            data = [edge[n * BE:(n + 1) * BE].reshape(1, 1, BE, C) for n in range(first, first + BLK_DEV)]
            regions.append((other, end, data, tags_of(ref, FACE + 2 * EDGE + side * TAG)))

    for i, s in enumerate(slots):
        here = pos_ref[s].astype(jnp.float32)
        for xs, ys, data, tags in regions:
            delta = [tag - here for tag in tags]
            for o3 in range(3):
                picks = []
                for n in range(BLK_DEV):
                    if o3 == 0:
                        wanted = jnp.where(row == 0, -1.0, 0.0)
                        moved = pltpu.roll(data[n].reshape(-1, BE, C), 1, 1)
                    elif o3 == 2:
                        wanted = jnp.where(row == BE - 1, 1.0, 0.0)
                        moved = pltpu.roll(data[n].reshape(-1, BE, C), BE - 1, 1)
                    else:
                        wanted = jnp.zeros((BE, C), jnp.float32)
                        moved = data[n].reshape(-1, BE, C)
                    picks.append(((delta[n] == wanted)[None], moved))
                value = jnp.where(picks[1][0], picks[1][1], 0.0)
                value = jnp.where(picks[0][0], picks[0][1], value)
                z_ref[o3, xs, ys] = value.reshape(data[0].shape)
        for o2 in range(3):
            for o3 in range(3):
                j = o2 * 3 + o3
                piece = z_ref[o3, :, o2:o2 + BE].reshape(SLAB, C)
                a_ref[i, :, j * C:(j + 1) * C] = piece.astype(jnp.bfloat16)


def wgrad_kernel(scale, pos_ref, core_ref, in_ref, g_ref, *refs):
    halo, keep_ref, send_ref, z_ref, a_ref, total_ref = refs[:4], *refs[-5:]
    fill_windows(1, (0, 1), pos_ref, g_ref, halo[0:2], halo[2:4], z_ref, a_ref)
    inner = [
        jnp.transpose(in_ref[s * VOX:(s + 1) * VOX, :].astype(jnp.float32)).astype(jnp.bfloat16)
        for s in range(BLK_DEV)
    ]
    total_ref[KV * C:, :] = jnp.zeros((2 * HALF - KV * C, C), jnp.float32)
    for e1 in range(3):
        rows = slice(e1 * BE * BE, e1 * BE * BE + VOX)
        total = jnp.dot(inner[0], a_ref[0, rows, :], preferred_element_type=jnp.float32)
        total = total + jnp.dot(inner[1], a_ref[1, rows, :], preferred_element_type=jnp.float32)
        total = total * scale
        for j in range(9):
            k = KV - 1 - (9 * e1 + j)
            total_ref[k * C:(k + 1) * C, :] = total[:, j * C:(j + 1) * C]
    core = core_ref[0]
    keep_ref[...] = total_ref[pl.ds(pl.multiple_of(core * HALF, HALF), HALF), :]
    send_ref[...] = total_ref[pl.ds(pl.multiple_of((1 - core) * HALF, HALF), HALF), :]


def coded(value):
    top = jnp.maximum(jnp.max(jnp.abs(value), axis=0, keepdims=True), 2.0 ** -120)
    exponent = jnp.floor(jnp.log2(top)) + 1.0
    steps = jnp.floor(value * (jnp.exp2(-exponent) * STEPS) + 0.5)
    last = jnp.broadcast_to(exponent, (TAG, C))
    return jnp.concatenate([steps, last]).astype(jnp.int32).astype(jnp.int16)


def decoded(ref, block=0):
    code = ref[block * CODED:(block + 1) * CODED, :].astype(jnp.int32).astype(jnp.float32)
    return code[:CHUNK] * (jnp.exp2(code[CHUNK:CHUNK + 1]) * (1.0 / STEPS))


def place_kernel(core_ref, near_ref, far_ref, out_ref):
    first = core_ref[0] == 0
    for block in range(16):
        near, far = decoded(near_ref, block), decoded(far_ref, block)
        at = block * CHUNK
        out_ref[at:at + CHUNK, :] = jnp.where(first, near, far)
        size = min(CHUNK, KV * C - HALF - at)
        if size > 0:
            out_ref[HALF + at:HALF + at + size, :] = jnp.where(first, far, near)[:size]


def turn_kernel(w_ref, out_ref, done_ref):
    for k in range(KV):
        at = (KV - 1 - k) * C
        out_ref[at:at + C, :] = jnp.transpose(w_ref[k * C:(k + 1) * C, :].astype(jnp.float32)).astype(jnp.bfloat16)
    done_ref[...] = jnp.zeros_like(done_ref)


def conv_kernel(field, slot, pos_ref, own_ref, mask_ref, w_ref, *refs):
    halo, out_ref, done_ref, z_ref, a_ref = refs[:4], *refs[-4:]
    fill_windows(field, (slot,), pos_ref, own_ref, halo[0:2], halo[2:4], z_ref, a_ref)
    total = None
    for e1 in range(3):
        rows = slice(e1 * BE * BE, e1 * BE * BE + VOX)
        part = jnp.dot(
            a_ref[0, rows, :], w_ref[e1 * SIDE:(e1 + 1) * SIDE, :], preferred_element_type=jnp.float32
        )
        total = part if total is None else total + part
    mask = mask_ref[slot * VOX:(slot + 1) * VOX, :].astype(jnp.float32)
    out_ref[0] = jnp.where(mask > 0, total, 0.0).astype(jnp.bfloat16)
    done_ref[...] = jnp.zeros_like(done_ref)


VMEM = pl.BlockSpec(memory_space=pltpu.VMEM)
ANY = pl.BlockSpec(memory_space=pl.ANY)
SMEM = pl.BlockSpec(memory_space=pltpu.SMEM)
PARAMS = pltpu.CompilerParams(vmem_limit_bytes=40 * 1024 * 1024)


def bf16(*shape):
    return jax.ShapeDtypeStruct(shape, jnp.bfloat16)


def prep(block_pos, occupancy, features, out_grad):
    field = pltpu.VMEM((BLK_DEV, VOX, C), jnp.bfloat16)
    return pl.pallas_call(
        prep_kernel,
        out_shape=[bf16(BLK_DEV * VOX, C)] * 3 + [bf16(FACE + TAG, C)] * 2,
        in_specs=[pl.BlockSpec(memory_space=pltpu.HBM)] * 4,
        out_specs=[VMEM] * 5,
        scratch_shapes=[
            pltpu.SMEM((BLK_DEV,), jnp.int32),
            pltpu.VMEM((BLK_DEV, VOX), jnp.int32),
            field,
            field,
            pltpu.SemaphoreType.DMA((4,)),
        ],
        compiler_params=PARAMS,
        name="mask_and_faces",
    )(block_pos, occupancy, features, out_grad)


def y_faces(block_pos, own_in, own_grad, low, high):
    return pl.pallas_call(
        y_faces_kernel,
        out_shape=[bf16(FACE + 2 * EDGE + 3 * TAG, C)] * 2,
        in_specs=[SMEM] + [VMEM] * 4,
        out_specs=[VMEM] * 2,
        compiler_params=PARAMS,
        name="y_faces",
    )(block_pos, own_in, own_grad, low, high)


def turn(weights, after):
    def kernel(w_ref, after_ref, *refs):
        turn_kernel(w_ref, *refs)

    return pl.pallas_call(
        kernel,
        out_shape=[bf16(KV * C, C), jax.ShapeDtypeStruct((BE, C), jnp.float32)],
        in_specs=[VMEM, ANY],
        out_specs=[VMEM] * 2,
        compiler_params=PARAMS,
        name="turn_weights",
    )(weights, after)


def scratch(slots):
    return [
        pltpu.VMEM((3, WIN, WIN, BE, C), jnp.float32),
        pltpu.VMEM((slots, SLAB, SIDE), jnp.bfloat16),
    ]


def wgrad(scale, block_pos, core, own_in, own_grad, halo, after):
    def kernel(*refs):
        wgrad_kernel(scale, *refs)

    half = jax.ShapeDtypeStruct((HALF, C), jnp.float32)
    return pl.pallas_call(
        kernel,
        out_shape=[half, half],
        in_specs=[SMEM] * 2 + [VMEM] * 6 + [ANY],
        out_specs=[VMEM] * 2,
        scratch_shapes=scratch(BLK_DEV) + [pltpu.VMEM((2 * HALF, C), jnp.float32)],
        compiler_params=PARAMS,
        name="kernel_gradient",
    )(block_pos, core, own_in, own_grad, *halo, after)


def place(core, near, far):
    return pl.pallas_call(
        place_kernel,
        out_shape=jax.ShapeDtypeStruct((KV * C, C), jnp.float32),
        in_specs=[SMEM] + [VMEM] * 2,
        out_specs=VMEM,
        compiler_params=PARAMS,
        name="place_halves",
    )(core, near, far)


def conv(field, slot, block_pos, own, mask, weights, halo, before, after):
    def kernel(*refs):
        conv_kernel(field, slot, *refs)

    flops = 2 * KV * VOX * C * C
    args = (block_pos, own, mask, weights, *halo)
    extra = ([] if before is None else [before]) + list(after)
    return pl.pallas_call(
        kernel,
        grid=(1,),
        out_shape=[bf16(BLK_DEV, VOX, C), jax.ShapeDtypeStruct((BE, C), jnp.float32)],
        in_specs=[SMEM] + [VMEM] * (len(args) - 1) + [ANY] * len(extra),
        out_specs=[pl.BlockSpec((1, VOX, C), lambda i: (slot, 0, 0)), VMEM],
        scratch_shapes=scratch(1),
        input_output_aliases={} if before is None else {len(args): 0},
        compiler_params=PARAMS,
        cost_estimate=pl.CostEstimate(flops=4 * flops, bytes_accessed=2_000_000, transcendentals=0),
        name=("convolution", "feature_gradient")[field],
    )(*args, *extra)


def small(kernel, outs, args, after=()):
    after = [v for v in after if v is not None]

    def inner(*refs):
        kernel(*refs[:len(args)], *refs[len(args) + len(after):])

    many = [jax.ShapeDtypeStruct((rows, C), jnp.int16) for rows in outs]
    return pl.pallas_call(
        inner,
        out_shape=many,
        in_specs=[VMEM] * len(args) + [ANY] * len(after),
        out_specs=[VMEM] * len(many),
        compiler_params=PARAMS,
        name=kernel.__name__.removesuffix("_kernel"),
    )(*args, *after)


def sum_halves_kernel(a_ref, b_ref, out_ref):
    for block in range(HALF // CHUNK):
        rows = slice(block * CHUNK, (block + 1) * CHUNK)
        out_ref[block * CODED:(block + 1) * CODED, :] = coded(a_ref[rows, :] + b_ref[rows, :])


def sum_blocks_kernel(*refs):
    *in_refs, out_ref = refs
    b = [decoded(ref, block) for ref in in_refs for block in range(ref.shape[0] // CODED)]
    while len(b) > 1:
        b = [b[i] + b[i + 1] for i in range(0, len(b), 2)]
    code = coded(b[0])
    for copy in range(out_ref.shape[0] // CODED):
        out_ref[copy * CODED:(copy + 1) * CODED, :] = code


def shifted(value, groups, tiles, up_g, up_t):
    pairs = [
        (g * tiles + t, (g + up_g) * tiles + t + up_t)
        for g in range(groups)
        for t in range(tiles)
        if 0 <= g + up_g < groups and 0 <= t + up_t < tiles
    ]
    return lax.ppermute(value, AXES, pairs)


def across(value, mask):
    count = lax.axis_size("group") * lax.axis_size("tile")
    return lax.ppermute(value, AXES, [(i, i ^ mask) for i in range(count)])


def exchange(value, axis, sets):
    count = len(sets[0])
    blocks = lax.all_to_all(value.reshape(count, -1, C), axis, 0, 0, axis_index_groups=sets)
    return blocks.reshape(-1, C)


def body(features, occupancy, block_pos, kernel, out_grad):
    groups, tiles = lax.axis_size("group"), lax.axis_size("tile")
    core = (lax.axis_index("tile") & 1).astype(jnp.int32).reshape(1)
    own_in, own_grad, mask, xlo, xhi = prep(block_pos, occupancy, features, out_grad)
    x_from = (shifted(xhi, groups, tiles, 1, 0), shifted(xlo, groups, tiles, -1, 0))
    ylo, yhi = y_faces(block_pos, own_in, own_grad, *x_from)
    y_from = (shifted(yhi, groups, tiles, 0, 1), shifted(ylo, groups, tiles, 0, -1))
    halo = (*x_from, *y_from)
    weights = kernel.reshape(KV * C, C)
    turned, done = turn(weights, yhi)
    scale = 1.0 / math.sqrt(groups * tiles * BLK_DEV * VOX)
    keep, send = wgrad(scale, block_pos, core, own_in, own_grad, halo, done)

    def convolved(field, slot, before, *after):
        return conv(
            field, slot, block_pos, (own_in, own_grad)[field], mask, (weights, turned)[field],
            halo, before, after,
        )

    got = across(send, CORE)
    conv_out, done = convolved(0, 0, None, send)
    value, = small(sum_halves_kernel, [16 * CODED], [keep, got], [done])
    value, = small(sum_blocks_kernel, [4 * CODED], [exchange(value, AXES, XY_SETS)])
    value, = small(sum_blocks_kernel, [CODED], [exchange(value, "tile", Z_LO_SETS)])
    got = across(value, Z_HI_BITS[0])
    conv_out, done = convolved(0, 1, conv_out, value)
    value, = small(sum_blocks_kernel, [CODED], [value, got], [done])
    got = across(value, Z_HI_BITS[1])
    feature_grad, done = convolved(1, 0, None, value)
    value, = small(sum_blocks_kernel, [16 * CODED], [value, got], [done])
    value = exchange(value, AXES, XY_SETS)
    got = across(value, CORE)
    feature_grad, done = convolved(1, 1, feature_grad, value)
    total = place(core, value, got)
    return (conv_out, feature_grad, total.reshape(KV, C, C))


def solution(mesh):
    in_specs = (
        P(AXES, None, None),
        P(AXES, None),
        P(AXES),
        P(),
        P(AXES, None, None),
    )
    out_specs = (P(AXES, None, None), P(AXES, None, None), P())
    return jax.shard_map(body, mesh=mesh, in_specs=in_specs, out_specs=out_specs, check_vma=False)
```

```python
import math

import jax
import jax.numpy as jnp
from jax import lax
from jax.experimental import pallas as pl
from jax.experimental.pallas import tpu as pltpu
from jax.sharding import PartitionSpec as P

BE = 8
VOX = 512
C = 128
KV = 27
BLK_DEV = 2
WIN = BE + 2
SLAB = WIN * BE * BE
SIDE = 9 * C
AXES = ("group", "tile")
FACE = 2 * BLK_DEV * BE * BE
EDGE = 2 * BLK_DEV * BE
TAG = 16
CHUNK = 112
CODED = CHUNK + TAG
STEPS = 32000.0
HALF = 16 * CHUNK
CORE = 1
XY_SETS = [
    [(y * 4 + z_hi) * 32 + z_lo * 8 + x * 2 + core for y in range(4) for x in range(4)]
    for z_hi in range(4) for z_lo in range(4) for core in range(2)
]
Z_LO_SETS = [[z * 8 + x * 2 + core for z in range(4)] for x in range(4) for core in range(2)]
Z_HI_BITS = (32, 96)


def tags(pos_ref):
    return jnp.concatenate(
        [jnp.full((BE, C), pos_ref[s].astype(jnp.float32), jnp.float32) for s in range(BLK_DEV)]
    ).astype(jnp.bfloat16)


def prep_kernel(*refs):
    sources, outs, held, sems = refs[:4], refs[4:11], refs[11:15], refs[15]
    in_ref, g_ref, mask_ref, xlo_ref, xhi_ref, ylo_ref, yhi_ref = outs
    copies = [pltpu.make_async_copy(src, dst, sems.at[i]) for i, (src, dst) in enumerate(zip(sources, held))]
    for copy in copies:
        copy.start()
    for copy in copies:
        copy.wait()
    pos_ref, occ_ref, feat_ref, grad_ref = held
    occ = occ_ref[...].astype(jnp.float32)
    layer = BE * BE
    for face in (xlo_ref, xhi_ref, ylo_ref, yhi_ref):
        face[FACE:FACE + TAG, :] = tags(pos_ref)
    for s in range(BLK_DEV):
        live = (pos_ref[s] >= 0).astype(jnp.float32)
        mask = jnp.concatenate([
            jnp.broadcast_to(occ[s:s + 1, r * C:(r + 1) * C] * live, (C, C)).T for r in range(VOX // C)
        ])
        mask_ref[s * VOX:(s + 1) * VOX, :] = mask.astype(jnp.bfloat16)
        for field, (src, dst) in enumerate(((feat_ref, in_ref), (grad_ref, g_ref))):
            value = jnp.where(mask > 0, src[s].astype(jnp.float32), 0.0)
            cube = value.reshape(BE, BE, BE, C)
            dst[s * VOX:(s + 1) * VOX, :] = value.astype(jnp.bfloat16)
            at = (field * BLK_DEV + s) * layer
            for face, piece in (
                (xlo_ref, cube[0]), (xhi_ref, cube[BE - 1]), (ylo_ref, cube[:, 0]), (yhi_ref, cube[:, BE - 1])
            ):
                face[at:at + layer, :] = piece.reshape(layer, C).astype(jnp.bfloat16)


def edges_kernel(low_ref, high_ref, after_ref, ylo_ref, yhi_ref):
    layer = BE * BE
    for side, ref in enumerate((low_ref, high_ref)):
        faces = [ref[n * layer:(n + 1) * layer, :].astype(jnp.float32) for n in range(2 * BLK_DEV)]
        for y, out in ((0, ylo_ref), (BE - 1, yhi_ref)):
            edge = [face[y * BE:(y + 1) * BE] for face in faces]
            out[side * EDGE:(side + 1) * EDGE, :] = jnp.concatenate(edge).astype(jnp.bfloat16)
            at = 2 * EDGE + side * TAG
            out[at:at + TAG, :] = ref[FACE:FACE + TAG, :]


def tags_of(ref, at):
    tag = ref[at:at + TAG, :].astype(jnp.float32)
    return [tag[0:BE], tag[BE:2 * BE]]


def face_of(ref, field, shape):
    first = field * BLK_DEV
    return [
        ref[n * BE * BE:(n + 1) * BE * BE, :].astype(jnp.float32).reshape(shape)
        for n in range(first, first + BLK_DEV)
    ]


def picked(data, their_tags, here, o3):
    row = lax.broadcasted_iota(jnp.int32, (BE, C), 0)
    value = jnp.zeros((), jnp.float32)
    for n in (1, 0):
        if o3 == 0:
            wanted, moved = jnp.where(row == 0, -1.0, 0.0), pltpu.roll(data[n], 1, 1)
        elif o3 == 2:
            wanted, moved = jnp.where(row == BE - 1, 1.0, 0.0), pltpu.roll(data[n], BE - 1, 1)
        else:
            wanted, moved = jnp.zeros((BE, C), jnp.float32), data[n]
        value = jnp.where(((their_tags[n] - here) == wanted)[None], moved, value)
    return value


def fill_windows(field, slots, pos_ref, own_ref, x_from, y_from, c_from, z_ref, a_ref):
    regions = []
    own = [own_ref[n * VOX:(n + 1) * VOX, :].astype(jnp.float32).reshape(BE, BE, BE, C) for n in range(BLK_DEV)]
    own_tags = [jnp.full((BE, C), pos_ref[n].astype(jnp.float32), jnp.float32) for n in range(BLK_DEV)]
    inside = slice(1, BE + 1)
    ends = (slice(0, 1), slice(WIN - 1, WIN))
    regions.append((inside, inside, own, own_tags))
    for ref, end in zip(x_from, ends):
        regions.append((end, inside, face_of(ref, field, (1, BE, BE, C)), tags_of(ref, FACE)))
    for ref, end in zip(y_from, ends):
        regions.append((inside, end, face_of(ref, field, (BE, 1, BE, C)), tags_of(ref, FACE)))
    for ref, end in zip(c_from, ends):
        for side, other in enumerate(ends):
            edge = ref[side * EDGE:(side + 1) * EDGE, :].astype(jnp.float32)
            first = field * BLK_DEV
            data = [edge[n * BE:(n + 1) * BE].reshape(1, 1, BE, C) for n in range(first, first + BLK_DEV)]
            regions.append((other, end, data, tags_of(ref, 2 * EDGE + side * TAG)))
    if not c_from:
        for x in ends:
            for y in ends:
                z_ref[:, x, y] = jnp.zeros((3, 1, 1, BE, C), jnp.float32)

    for i, s in enumerate(slots):
        here = pos_ref[s].astype(jnp.float32)
        for xs, ys, data, their_tags in regions:
            flat = [v.reshape(-1, BE, C) for v in data]
            for o3 in range(3):
                z_ref[o3, xs, ys] = picked(flat, their_tags, here, o3).reshape(data[0].shape)
        for o2 in range(3):
            for o3 in range(3):
                j = o2 * 3 + o3
                piece = z_ref[o3, :, o2:o2 + BE].reshape(SLAB, C)
                a_ref[i, :, j * C:(j + 1) * C] = piece.astype(jnp.bfloat16)


def diagonal_pairs(x_high, y_low, y_high):
    def column(ref, field, end):
        return [v[:, end] for v in face_of(ref, field, (1, BE, BE, C))]

    last = BE - 1
    plans = {
        0: (((x_high, 0), (y_low, last), 0), ((x_high, last), (y_high, last), 2)),
        2: (((y_low, last), (x_high, 0), 2), ((y_high, last), (x_high, last), 0)),
    }
    result = {}
    for e1, plan in plans.items():
        inputs, rows = [], []
        for (near, near_end), (far, far_end), e2 in plan:
            inputs += [v.reshape(BE, C) for v in column(near, 0, near_end)]
            data, their_tags = column(far, 1, far_end), tags_of(far, FACE)
            for here in tags_of(near, FACE):
                blank = jnp.zeros((BE, C), jnp.float32)
                lanes = [blank] * 9
                for e3 in range(3):
                    lanes[3 * e2 + e3] = picked(data, their_tags, here, e3).reshape(BE, C)
                rows.append(jnp.concatenate(lanes, axis=1))
        result[e1] = (jnp.concatenate(inputs), jnp.concatenate(rows).astype(jnp.bfloat16))
    return result


def wgrad_kernel(scale, pos_ref, core_ref, in_ref, g_ref, *refs):
    halo, keep_ref, send_ref, z_ref, a_ref, total_ref = refs[:4], *refs[-5:]
    fill_windows(1, (0, 1), pos_ref, g_ref, halo[0:2], halo[2:4], (), z_ref, a_ref)
    pairs = diagonal_pairs(halo[1], halo[2], halo[3])
    inner = [
        jnp.transpose(in_ref[s * VOX:(s + 1) * VOX, :].astype(jnp.float32)).astype(jnp.bfloat16)
        for s in range(BLK_DEV)
    ]
    total_ref[KV * C:, :] = jnp.zeros((2 * HALF - KV * C, C), jnp.float32)
    for e1 in range(3):
        rows = slice(e1 * BE * BE, e1 * BE * BE + VOX)
        total = jnp.dot(inner[0], a_ref[0, rows, :], preferred_element_type=jnp.float32)
        total = total + jnp.dot(inner[1], a_ref[1, rows, :], preferred_element_type=jnp.float32)
        if e1 in pairs:
            lhs, rhs = pairs[e1]
            lhs = jnp.concatenate([lhs, jnp.zeros((C - lhs.shape[0], C), jnp.float32)])
            rhs = jnp.concatenate([rhs, jnp.zeros((C - rhs.shape[0], SIDE), jnp.bfloat16)])
            total = total + jnp.dot(lhs.T.astype(jnp.bfloat16), rhs, preferred_element_type=jnp.float32)
        total = total * scale
        for j in range(9):
            k = KV - 1 - (9 * e1 + j)
            total_ref[k * C:(k + 1) * C, :] = total[:, j * C:(j + 1) * C]
    core = core_ref[0]
    keep_ref[...] = total_ref[pl.ds(pl.multiple_of(core * HALF, HALF), HALF), :]
    send_ref[...] = total_ref[pl.ds(pl.multiple_of((1 - core) * HALF, HALF), HALF), :]


def coded(value):
    top = jnp.maximum(jnp.max(jnp.abs(value), axis=0, keepdims=True), 2.0 ** -120)
    exponent = jnp.floor(jnp.log2(top)) + 1.0
    steps = jnp.floor(value * (jnp.exp2(-exponent) * STEPS) + 0.5)
    last = jnp.broadcast_to(exponent, (TAG, C))
    return jnp.concatenate([steps, last]).astype(jnp.int32).astype(jnp.int16)


def decoded(ref, block=0):
    code = ref[block * CODED:(block + 1) * CODED, :].astype(jnp.int32).astype(jnp.float32)
    return code[:CHUNK] * (jnp.exp2(code[CHUNK:CHUNK + 1]) * (1.0 / STEPS))


def place_kernel(core_ref, near_ref, far_ref, out_ref):
    first = core_ref[0] == 0
    for block in range(16):
        near, far = decoded(near_ref, block), decoded(far_ref, block)
        at = block * CHUNK
        out_ref[at:at + CHUNK, :] = jnp.where(first, near, far)
        size = min(CHUNK, KV * C - HALF - at)
        if size > 0:
            out_ref[HALF + at:HALF + at + size, :] = jnp.where(first, far, near)[:size]


def turn_kernel(w_ref, out_ref, done_ref):
    for k in range(KV):
        at = (KV - 1 - k) * C
        out_ref[at:at + C, :] = jnp.transpose(w_ref[k * C:(k + 1) * C, :].astype(jnp.float32)).astype(jnp.bfloat16)
    done_ref[...] = jnp.zeros_like(done_ref)


def conv_kernel(field, slot, pos_ref, own_ref, mask_ref, w_ref, *refs):
    halo, out_ref, done_ref, z_ref, a_ref = refs[:6], *refs[-4:]
    fill_windows(field, (slot,), pos_ref, own_ref, halo[0:2], halo[2:4], halo[4:6], z_ref, a_ref)
    total = None
    for e1 in range(3):
        rows = slice(e1 * BE * BE, e1 * BE * BE + VOX)
        part = jnp.dot(
            a_ref[0, rows, :], w_ref[e1 * SIDE:(e1 + 1) * SIDE, :], preferred_element_type=jnp.float32
        )
        total = part if total is None else total + part
    mask = mask_ref[slot * VOX:(slot + 1) * VOX, :].astype(jnp.float32)
    out_ref[0] = jnp.where(mask > 0, total, 0.0).astype(jnp.bfloat16)
    done_ref[...] = jnp.zeros_like(done_ref)


VMEM = pl.BlockSpec(memory_space=pltpu.VMEM)
ANY = pl.BlockSpec(memory_space=pl.ANY)
SMEM = pl.BlockSpec(memory_space=pltpu.SMEM)
PARAMS = pltpu.CompilerParams(vmem_limit_bytes=40 * 1024 * 1024)


def bf16(*shape):
    return jax.ShapeDtypeStruct(shape, jnp.bfloat16)


def prep(block_pos, occupancy, features, out_grad):
    field = pltpu.VMEM((BLK_DEV, VOX, C), jnp.bfloat16)
    return pl.pallas_call(
        prep_kernel,
        out_shape=[bf16(BLK_DEV * VOX, C)] * 3 + [bf16(FACE + TAG, C)] * 4,
        in_specs=[pl.BlockSpec(memory_space=pltpu.HBM)] * 4,
        out_specs=[VMEM] * 7,
        scratch_shapes=[
            pltpu.SMEM((BLK_DEV,), jnp.int32),
            pltpu.VMEM((BLK_DEV, VOX), jnp.int32),
            field,
            field,
            pltpu.SemaphoreType.DMA((4,)),
        ],
        compiler_params=PARAMS,
        name="mask_and_faces",
    )(block_pos, occupancy, features, out_grad)


def edges(low, high, after):
    return pl.pallas_call(
        edges_kernel,
        out_shape=[bf16(2 * EDGE + 2 * TAG, C)] * 2,
        in_specs=[VMEM] * 2 + [ANY],
        out_specs=[VMEM] * 2,
        compiler_params=PARAMS,
        name="edges",
    )(low, high, after)


def turn(weights, after):
    def kernel(w_ref, after_ref, *refs):
        turn_kernel(w_ref, *refs)

    return pl.pallas_call(
        kernel,
        out_shape=[bf16(KV * C, C), jax.ShapeDtypeStruct((BE, C), jnp.float32)],
        in_specs=[VMEM, ANY],
        out_specs=[VMEM] * 2,
        compiler_params=PARAMS,
        name="turn_weights",
    )(weights, after)


def scratch(slots):
    return [
        pltpu.VMEM((3, WIN, WIN, BE, C), jnp.float32),
        pltpu.VMEM((slots, SLAB, SIDE), jnp.bfloat16),
    ]


def wgrad(scale, block_pos, core, own_in, own_grad, halo, after):
    def kernel(*refs):
        wgrad_kernel(scale, *refs)

    half = jax.ShapeDtypeStruct((HALF, C), jnp.float32)
    return pl.pallas_call(
        kernel,
        out_shape=[half, half],
        in_specs=[SMEM] * 2 + [VMEM] * 6 + [ANY],
        out_specs=[VMEM] * 2,
        scratch_shapes=scratch(BLK_DEV) + [pltpu.VMEM((2 * HALF, C), jnp.float32)],
        compiler_params=PARAMS,
        name="kernel_gradient",
    )(block_pos, core, own_in, own_grad, *halo, after)


def place(core, near, far):
    return pl.pallas_call(
        place_kernel,
        out_shape=jax.ShapeDtypeStruct((KV * C, C), jnp.float32),
        in_specs=[SMEM] + [VMEM] * 2,
        out_specs=VMEM,
        compiler_params=PARAMS,
        name="place_halves",
    )(core, near, far)


def conv(field, slot, block_pos, own, mask, weights, halo, before, after):
    def kernel(*refs):
        conv_kernel(field, slot, *refs)

    flops = 2 * KV * VOX * C * C
    args = (block_pos, own, mask, weights, *halo)
    extra = ([] if before is None else [before]) + list(after)
    return pl.pallas_call(
        kernel,
        grid=(1,),
        out_shape=[bf16(BLK_DEV, VOX, C), jax.ShapeDtypeStruct((BE, C), jnp.float32)],
        in_specs=[SMEM] + [VMEM] * (len(args) - 1) + [ANY] * len(extra),
        out_specs=[pl.BlockSpec((1, VOX, C), lambda i: (slot, 0, 0)), VMEM],
        scratch_shapes=scratch(1),
        input_output_aliases={} if before is None else {len(args): 0},
        compiler_params=PARAMS,
        cost_estimate=pl.CostEstimate(flops=4 * flops, bytes_accessed=2_000_000, transcendentals=0),
        name=("convolution", "feature_gradient")[field],
    )(*args, *extra)


def small(kernel, outs, args, after=()):
    after = [v for v in after if v is not None]

    def inner(*refs):
        kernel(*refs[:len(args)], *refs[len(args) + len(after):])

    many = [jax.ShapeDtypeStruct((rows, C), jnp.int16) for rows in outs]
    return pl.pallas_call(
        inner,
        out_shape=many,
        in_specs=[VMEM] * len(args) + [ANY] * len(after),
        out_specs=[VMEM] * len(many),
        compiler_params=PARAMS,
        name=kernel.__name__.removesuffix("_kernel"),
    )(*args, *after)


def sum_halves_kernel(a_ref, b_ref, out_ref):
    for block in range(HALF // CHUNK):
        rows = slice(block * CHUNK, (block + 1) * CHUNK)
        out_ref[block * CODED:(block + 1) * CODED, :] = coded(a_ref[rows, :] + b_ref[rows, :])


def sum_blocks_kernel(*refs):
    *in_refs, out_ref = refs
    b = [decoded(ref, block) for ref in in_refs for block in range(ref.shape[0] // CODED)]
    while len(b) > 1:
        b = [b[i] + b[i + 1] for i in range(0, len(b), 2)]
    code = coded(b[0])
    for copy in range(out_ref.shape[0] // CODED):
        out_ref[copy * CODED:(copy + 1) * CODED, :] = code


def shifted(value, groups, tiles, up_g, up_t):
    pairs = [
        (g * tiles + t, (g + up_g) * tiles + t + up_t)
        for g in range(groups)
        for t in range(tiles)
        if 0 <= g + up_g < groups and 0 <= t + up_t < tiles
    ]
    return lax.ppermute(value, AXES, pairs)


def across(value, mask):
    count = lax.axis_size("group") * lax.axis_size("tile")
    return lax.ppermute(value, AXES, [(i, i ^ mask) for i in range(count)])


def exchange(value, axis, sets):
    count = len(sets[0])
    blocks = lax.all_to_all(value.reshape(count, -1, C), axis, 0, 0, axis_index_groups=sets)
    return blocks.reshape(-1, C)


def body(features, occupancy, block_pos, kernel, out_grad):
    groups, tiles = lax.axis_size("group"), lax.axis_size("tile")
    core = (lax.axis_index("tile") & 1).astype(jnp.int32).reshape(1)
    own_in, own_grad, mask, xlo, xhi, ylo, yhi = prep(block_pos, occupancy, features, out_grad)
    x_from = (shifted(xhi, groups, tiles, 1, 0), shifted(xlo, groups, tiles, -1, 0))
    y_from = (shifted(yhi, groups, tiles, 0, 1), shifted(ylo, groups, tiles, 0, -1))
    halo = (*x_from, *y_from)
    weights = kernel.reshape(KV * C, C)
    turned, done = turn(weights, yhi)
    scale = 1.0 / math.sqrt(groups * tiles * BLK_DEV * VOX)
    keep, send = wgrad(scale, block_pos, core, own_in, own_grad, halo, done)

    def convolved(field, slot, before, *after):
        return conv(
            field, slot, block_pos, (own_in, own_grad)[field], mask, (weights, turned)[field],
            halo, before, after,
        )

    got = across(send, CORE)
    clo, chi = edges(*x_from, send)
    halo += (shifted(chi, groups, tiles, 0, 1), shifted(clo, groups, tiles, 0, -1))
    value, = small(sum_halves_kernel, [16 * CODED], [keep, got], [clo])
    value, = small(sum_blocks_kernel, [4 * CODED], [exchange(value, AXES, XY_SETS)])
    value, = small(sum_blocks_kernel, [CODED], [exchange(value, "tile", Z_LO_SETS)])
    got = across(value, Z_HI_BITS[0])
    conv_out, done = convolved(0, 0, None, value)
    conv_out, done = convolved(0, 1, conv_out, done)
    value, = small(sum_blocks_kernel, [CODED], [value, got], [done])
    got = across(value, Z_HI_BITS[1])
    feature_grad, done = convolved(1, 0, None, value)
    value, = small(sum_blocks_kernel, [16 * CODED], [value, got], [done])
    value = exchange(value, AXES, XY_SETS)
    got = across(value, CORE)
    feature_grad, done = convolved(1, 1, feature_grad, value)
    total = place(core, value, got)
    return (conv_out, feature_grad, total.reshape(KV, C, C))


def solution(mesh):
    in_specs = (
        P(AXES, None, None),
        P(AXES, None),
        P(AXES),
        P(),
        P(AXES, None, None),
    )
    out_specs = (P(AXES, None, None), P(AXES, None, None), P())
    return jax.shard_map(body, mesh=mesh, in_specs=in_specs, out_specs=out_specs, check_vma=False)
```

```python
import math

import jax
import jax.numpy as jnp
from jax import lax
from jax.experimental import pallas as pl
from jax.experimental.pallas import tpu as pltpu
from jax.sharding import PartitionSpec as P

BE = 8
VOX = 512
C = 128
KV = 27
BLK_DEV = 2
WIN = BE + 2
SLAB = WIN * BE * BE
SIDE = 9 * C
AXES = ("group", "tile")
FACE = 2 * BLK_DEV * BE * BE
EDGE = 2 * BLK_DEV * BE
TAG = 16
CHUNK = 112
CODED = CHUNK + TAG
STEPS = 32000.0
HALF = 16 * CHUNK
CORE = 1
XY_SETS = [
    [(y * 4 + z_hi) * 32 + z_lo * 8 + x * 2 + core for y in range(4) for x in range(4)]
    for z_hi in range(4) for z_lo in range(4) for core in range(2)
]
Z_LO_SETS = [[z * 8 + x * 2 + core for z in range(4)] for x in range(4) for core in range(2)]
Z_HI_BITS = (32, 96)


def prep_kernel(*refs):
    sources, outs, held, sems = refs[:4], refs[4:12], refs[12:16], refs[16]
    in_ref, g_ref, mask_ref, tag_ref, xlo_ref, xhi_ref, ylo_ref, yhi_ref = outs
    copies = [pltpu.make_async_copy(src, dst, sems.at[i]) for i, (src, dst) in enumerate(zip(sources, held))]
    for copy in copies:
        copy.start()
    for copy in copies:
        copy.wait()
    pos_ref, occ_ref, feat_ref, grad_ref = held
    occ = occ_ref[...].astype(jnp.float32)
    layer = BE * BE
    tag = jnp.concatenate(
        [jnp.full((BE, C), pos_ref[s].astype(jnp.float32), jnp.float32) for s in range(BLK_DEV)]
    ).astype(jnp.bfloat16)
    tag_ref[...] = tag
    for face in (xlo_ref, xhi_ref, ylo_ref, yhi_ref):
        face[FACE:FACE + TAG, :] = tag
    for s in range(BLK_DEV):
        live = (pos_ref[s] >= 0).astype(jnp.float32)
        mask = jnp.concatenate([
            jnp.broadcast_to(occ[s:s + 1, r * C:(r + 1) * C] * live, (C, C)).T for r in range(VOX // C)
        ])
        mask_ref[s * VOX:(s + 1) * VOX, :] = mask.astype(jnp.bfloat16)
        for field, (src, dst) in enumerate(((feat_ref, in_ref), (grad_ref, g_ref))):
            value = jnp.where(mask > 0, src[s].astype(jnp.float32), 0.0)
            cube = value.reshape(BE, BE, BE, C)
            dst[s * VOX:(s + 1) * VOX, :] = value.astype(jnp.bfloat16)
            at = (field * BLK_DEV + s) * layer
            for face, piece in (
                (xlo_ref, cube[0]), (xhi_ref, cube[BE - 1]), (ylo_ref, cube[:, 0]), (yhi_ref, cube[:, BE - 1])
            ):
                face[at:at + layer, :] = piece.reshape(layer, C).astype(jnp.bfloat16)


def edges_kernel(low_ref, high_ref, ylo_ref, yhi_ref):
    layer = BE * BE
    for side, ref in enumerate((low_ref, high_ref)):
        faces = [ref[n * layer:(n + 1) * layer, :].astype(jnp.float32) for n in range(2 * BLK_DEV)]
        for y, out in ((0, ylo_ref), (BE - 1, yhi_ref)):
            edge = [face[y * BE:(y + 1) * BE] for face in faces]
            out[side * EDGE:(side + 1) * EDGE, :] = jnp.concatenate(edge).astype(jnp.bfloat16)
            at = 2 * EDGE + side * TAG
            out[at:at + TAG, :] = ref[FACE:FACE + TAG, :]


def tags_of(ref, at):
    tag = ref[at:at + TAG, :].astype(jnp.float32)
    return [tag[0:BE], tag[BE:2 * BE]]


def face_of(ref, field, shape):
    first = field * BLK_DEV
    return [
        ref[n * BE * BE:(n + 1) * BE * BE, :].astype(jnp.float32).reshape(shape)
        for n in range(first, first + BLK_DEV)
    ]


def picked(data, their_tags, here, o3):
    row = lax.broadcasted_iota(jnp.int32, (BE, C), 0)
    value = jnp.zeros((), jnp.float32)
    for n in (1, 0):
        if o3 == 0:
            wanted, moved = jnp.where(row == 0, -1.0, 0.0), pltpu.roll(data[n], 1, 1)
        elif o3 == 2:
            wanted, moved = jnp.where(row == BE - 1, 1.0, 0.0), pltpu.roll(data[n], BE - 1, 1)
        else:
            wanted, moved = jnp.zeros((BE, C), jnp.float32), data[n]
        value = jnp.where(((their_tags[n] - here) == wanted)[None], moved, value)
    return value


def fill_windows(field, slots, tag_ref, own_ref, x_from, y_from, c_from, z_ref, a_ref):
    regions = []
    own = [own_ref[n * VOX:(n + 1) * VOX, :].astype(jnp.float32).reshape(BE, BE, BE, C) for n in range(BLK_DEV)]
    own_tags = tags_of(tag_ref, 0)
    inside = slice(1, BE + 1)
    ends = (slice(0, 1), slice(WIN - 1, WIN))
    regions.append((inside, inside, own, own_tags))
    for ref, end in zip(x_from, ends):
        if ref is None:
            z_ref[:, end, inside] = jnp.zeros((3, 1, BE, BE, C), jnp.float32)
            continue
        regions.append((end, inside, face_of(ref, field, (1, BE, BE, C)), tags_of(ref, FACE)))
    for ref, end in zip(y_from, ends):
        regions.append((inside, end, face_of(ref, field, (BE, 1, BE, C)), tags_of(ref, FACE)))
    for ref, end in zip(c_from, ends):
        for side, other in enumerate(ends):
            edge = ref[side * EDGE:(side + 1) * EDGE, :].astype(jnp.float32)
            first = field * BLK_DEV
            data = [edge[n * BE:(n + 1) * BE].reshape(1, 1, BE, C) for n in range(first, first + BLK_DEV)]
            regions.append((other, end, data, tags_of(ref, 2 * EDGE + side * TAG)))
    if not c_from:
        for x in ends:
            for y in ends:
                z_ref[:, x, y] = jnp.zeros((3, 1, 1, BE, C), jnp.float32)

    for i, s in enumerate(slots):
        here = own_tags[s]
        for xs, ys, data, their_tags in regions:
            flat = [v.reshape(-1, BE, C) for v in data]
            for o3 in range(3):
                z_ref[o3, xs, ys] = picked(flat, their_tags, here, o3).reshape(data[0].shape)
        for o2 in range(3):
            for o3 in range(3):
                j = o2 * 3 + o3
                piece = z_ref[o3, :, o2:o2 + BE].reshape(SLAB, C)
                a_ref[i, :, j * C:(j + 1) * C] = piece.astype(jnp.bfloat16)


def lower_pairs(tag_ref, g_ref, x_low, y_low, y_high):
    last = BE - 1
    blank = jnp.zeros((1, BE, C), jnp.float32)

    def column(ref, field, end):
        return [v[:, end] for v in face_of(ref, field, (1, BE, BE, C))]

    inputs, rows = {0: [], 2: []}, {0: [], 2: []}
    own_tags = tags_of(tag_ref, 0)
    plane = [
        g_ref[n * VOX:n * VOX + BE * BE, :].astype(jnp.float32).reshape(BE, BE, C) for n in range(BLK_DEV)
    ]
    inputs[2] += face_of(x_low, 0, (BE * BE, C))
    for here in tags_of(x_low, FACE):
        lanes = []
        above = [
            jnp.concatenate([blank, picked(plane, own_tags, here, e3), blank]) for e3 in range(3)
        ]
        for e2 in range(3):
            lanes += [above[e3][e2:e2 + BE].reshape(BE * BE, C) for e3 in range(3)]
        rows[2].append(jnp.concatenate(lanes, axis=1))
    plans = (
        (2, 2, (x_low, last), (y_high, 0)),
        (2, 0, (x_low, 0), (y_low, 0)),
        (0, 0, (y_high, 0), (x_low, last)),
        (0, 2, (y_low, 0), (x_low, 0)),
    )
    for e1, e2, (near, near_end), (far, far_end) in plans:
        inputs[e1] += [v.reshape(BE, C) for v in column(near, 0, near_end)]
        data, their_tags = column(far, 1, far_end), tags_of(far, FACE)
        for here in tags_of(near, FACE):
            lanes = [blank.reshape(BE, C)] * 9
            for e3 in range(3):
                lanes[3 * e2 + e3] = picked(data, their_tags, here, e3).reshape(BE, C)
            rows[e1].append(jnp.concatenate(lanes, axis=1))
    result = {}
    for e1 in inputs:
        lhs, rhs = jnp.concatenate(inputs[e1]), jnp.concatenate(rows[e1])
        more = -lhs.shape[0] % C
        lhs = jnp.concatenate([lhs, jnp.zeros((more, C), jnp.float32)])
        rhs = jnp.concatenate([rhs, jnp.zeros((more, SIDE), jnp.float32)])
        result[e1] = (lhs.T.astype(jnp.bfloat16), rhs.astype(jnp.bfloat16))
    return result


def wgrad_kernel(scale, tag_ref, core_ref, in_ref, g_ref, *refs):
    halo, keep_ref, send_ref, z_ref, a_ref, total_ref = refs[:3], *refs[-5:]
    fill_windows(1, (0, 1), tag_ref, g_ref, (halo[0], None), halo[1:3], (), z_ref, a_ref)
    pairs = lower_pairs(tag_ref, g_ref, *halo)
    inner = [
        jnp.transpose(in_ref[s * VOX:(s + 1) * VOX, :].astype(jnp.float32)).astype(jnp.bfloat16)
        for s in range(BLK_DEV)
    ]
    total_ref[KV * C:, :] = jnp.zeros((2 * HALF - KV * C, C), jnp.float32)
    for e1 in range(3):
        rows = slice(e1 * BE * BE, e1 * BE * BE + VOX)
        total = jnp.dot(inner[0], a_ref[0, rows, :], preferred_element_type=jnp.float32)
        total = total + jnp.dot(inner[1], a_ref[1, rows, :], preferred_element_type=jnp.float32)
        if e1 in pairs:
            total = total + jnp.dot(*pairs[e1], preferred_element_type=jnp.float32)
        total = total * scale
        for j in range(9):
            k = KV - 1 - (9 * e1 + j)
            total_ref[k * C:(k + 1) * C, :] = total[:, j * C:(j + 1) * C]
    core = core_ref[0]
    keep_ref[...] = total_ref[pl.ds(pl.multiple_of(core * HALF, HALF), HALF), :]
    send_ref[...] = total_ref[pl.ds(pl.multiple_of((1 - core) * HALF, HALF), HALF), :]


def coded(value):
    top = jnp.maximum(jnp.max(jnp.abs(value), axis=0, keepdims=True), 2.0 ** -120)
    exponent = jnp.floor(jnp.log2(top)) + 1.0
    steps = jnp.floor(value * (jnp.exp2(-exponent) * STEPS) + 0.5)
    last = jnp.broadcast_to(exponent, (TAG, C))
    return jnp.concatenate([steps, last]).astype(jnp.int32).astype(jnp.int16)


def decoded(ref, block=0):
    code = ref[block * CODED:(block + 1) * CODED, :].astype(jnp.int32).astype(jnp.float32)
    return code[:CHUNK] * (jnp.exp2(code[CHUNK:CHUNK + 1]) * (1.0 / STEPS))


def place_kernel(core_ref, near_ref, far_ref, after_ref, out_ref):
    first = core_ref[0] == 0
    for block in range(16):
        near, far = decoded(near_ref, block), decoded(far_ref, block)
        at = block * CHUNK
        out_ref[at:at + CHUNK, :] = jnp.where(first, near, far)
        size = min(CHUNK, KV * C - HALF - at)
        if size > 0:
            out_ref[HALF + at:HALF + at + size, :] = jnp.where(first, far, near)[:size]


def turn_kernel(w_ref, out_ref, done_ref):
    for k in range(KV):
        at = (KV - 1 - k) * C
        out_ref[at:at + C, :] = jnp.transpose(w_ref[k * C:(k + 1) * C, :].astype(jnp.float32)).astype(jnp.bfloat16)
    done_ref[...] = jnp.zeros_like(done_ref)


def conv_kernel(field, slot, tag_ref, own_ref, mask_ref, w_ref, *refs):
    halo, out_ref, done_ref, z_ref, a_ref = refs[:6], *refs[-4:]
    fill_windows(field, (slot,), tag_ref, own_ref, halo[0:2], halo[2:4], halo[4:6], z_ref, a_ref)
    total = None
    for e1 in range(3):
        rows = slice(e1 * BE * BE, e1 * BE * BE + VOX)
        part = jnp.dot(
            a_ref[0, rows, :], w_ref[e1 * SIDE:(e1 + 1) * SIDE, :], preferred_element_type=jnp.float32
        )
        total = part if total is None else total + part
    mask = mask_ref[slot * VOX:(slot + 1) * VOX, :].astype(jnp.float32)
    out_ref[0] = jnp.where(mask > 0, total, 0.0).astype(jnp.bfloat16)
    done_ref[...] = jnp.zeros_like(done_ref)


VMEM = pl.BlockSpec(memory_space=pltpu.VMEM)
ANY = pl.BlockSpec(memory_space=pl.ANY)
SMEM = pl.BlockSpec(memory_space=pltpu.SMEM)
PARAMS = pltpu.CompilerParams(vmem_limit_bytes=40 * 1024 * 1024)


def bf16(*shape):
    return jax.ShapeDtypeStruct(shape, jnp.bfloat16)


def prep(block_pos, occupancy, features, out_grad):
    field = pltpu.VMEM((BLK_DEV, VOX, C), jnp.bfloat16)
    return pl.pallas_call(
        prep_kernel,
        out_shape=[bf16(BLK_DEV * VOX, C)] * 3 + [bf16(TAG, C)] + [bf16(FACE + TAG, C)] * 4,
        in_specs=[pl.BlockSpec(memory_space=pltpu.HBM)] * 4,
        out_specs=[VMEM] * 8,
        scratch_shapes=[
            pltpu.SMEM((BLK_DEV,), jnp.int32),
            pltpu.VMEM((BLK_DEV, VOX), jnp.int32),
            field,
            field,
            pltpu.SemaphoreType.DMA((4,)),
        ],
        compiler_params=PARAMS,
        name="mask_and_faces",
    )(*[pltpu.with_memory_space_constraint(v, pltpu.HBM) for v in (block_pos, occupancy, features, out_grad)])


def edges(low, high):
    return pl.pallas_call(
        edges_kernel,
        out_shape=[bf16(2 * EDGE + 2 * TAG, C)] * 2,
        in_specs=[VMEM] * 2,
        out_specs=[VMEM] * 2,
        compiler_params=PARAMS,
        name="edges",
    )(low, high)


def turn(weights, after):
    def kernel(w_ref, after_ref, *refs):
        turn_kernel(w_ref, *refs)

    return pl.pallas_call(
        kernel,
        out_shape=[bf16(KV * C, C), jax.ShapeDtypeStruct((BE, C), jnp.float32)],
        in_specs=[VMEM, ANY],
        out_specs=[VMEM] * 2,
        compiler_params=PARAMS,
        name="turn_weights",
    )(weights, after)


def scratch(slots):
    return [
        pltpu.VMEM((3, WIN, WIN, BE, C), jnp.float32),
        pltpu.VMEM((slots, SLAB, SIDE), jnp.bfloat16),
    ]


def wgrad(scale, tag, core, own_in, own_grad, halo, *after):
    def kernel(*refs):
        wgrad_kernel(scale, *refs)

    half = jax.ShapeDtypeStruct((HALF, C), jnp.float32)
    return pl.pallas_call(
        kernel,
        out_shape=[half, half],
        in_specs=[VMEM, SMEM] + [VMEM] * 5 + [ANY] * len(after),
        out_specs=[VMEM] * 2,
        scratch_shapes=scratch(BLK_DEV) + [pltpu.VMEM((2 * HALF, C), jnp.float32)],
        compiler_params=PARAMS,
        name="kernel_gradient",
    )(tag, core, own_in, own_grad, *halo, *after)


def place(core, near, far, after):
    return pl.pallas_call(
        place_kernel,
        out_shape=jax.ShapeDtypeStruct((KV * C, C), jnp.float32),
        in_specs=[SMEM] + [VMEM] * 2 + [ANY],
        out_specs=VMEM,
        compiler_params=PARAMS,
        name="place_halves",
    )(core, near, far, after)


def conv(field, slot, tag, own, mask, weights, halo, before, after):
    def kernel(*refs):
        conv_kernel(field, slot, *refs)

    flops = 2 * KV * VOX * C * C
    args = (tag, own, mask, weights, *halo)
    extra = ([] if before is None else [before]) + list(after)
    return pl.pallas_call(
        kernel,
        grid=(1,),
        out_shape=[bf16(BLK_DEV, VOX, C), jax.ShapeDtypeStruct((BE, C), jnp.float32)],
        in_specs=[VMEM] * len(args) + [ANY] * len(extra),
        out_specs=[pl.BlockSpec((1, VOX, C), lambda i: (slot, 0, 0)), VMEM],
        scratch_shapes=scratch(1),
        input_output_aliases={} if before is None else {len(args): 0},
        compiler_params=PARAMS,
        cost_estimate=pl.CostEstimate(flops=4 * flops, bytes_accessed=2_000_000, transcendentals=0),
        name=("convolution", "feature_gradient")[field],
    )(*args, *extra)


def small(kernel, outs, args, after=()):
    after = [v for v in after if v is not None]

    def inner(*refs):
        kernel(*refs[:len(args)], *refs[len(args) + len(after):])

    many = [jax.ShapeDtypeStruct((rows, C), jnp.int16) for rows in outs]
    return pl.pallas_call(
        inner,
        out_shape=many,
        in_specs=[VMEM] * len(args) + [ANY] * len(after),
        out_specs=[VMEM] * len(many),
        compiler_params=PARAMS,
        name=kernel.__name__.removesuffix("_kernel"),
    )(*args, *after)


def sum_halves_kernel(a_ref, b_ref, out_ref):
    for block in range(HALF // CHUNK):
        rows = slice(block * CHUNK, (block + 1) * CHUNK)
        out_ref[block * CODED:(block + 1) * CODED, :] = coded(a_ref[rows, :] + b_ref[rows, :])


def sum_blocks_kernel(*refs):
    *in_refs, out_ref = refs
    b = [decoded(ref, block) for ref in in_refs for block in range(ref.shape[0] // CODED)]
    while len(b) > 1:
        b = [b[i] + b[i + 1] for i in range(0, len(b), 2)]
    code = coded(b[0])
    for copy in range(out_ref.shape[0] // CODED):
        out_ref[copy * CODED:(copy + 1) * CODED, :] = code


def shifted(value, groups, tiles, up_g, up_t):
    pairs = [
        (g * tiles + t, (g + up_g) * tiles + t + up_t)
        for g in range(groups)
        for t in range(tiles)
        if 0 <= g + up_g < groups and 0 <= t + up_t < tiles
    ]
    return lax.ppermute(value, AXES, pairs)


def across(value, mask):
    count = lax.axis_size("group") * lax.axis_size("tile")
    return lax.ppermute(value, AXES, [(i, i ^ mask) for i in range(count)])


def exchange(value, axis, sets):
    count = len(sets[0])
    blocks = lax.all_to_all(value.reshape(count, -1, C), axis, 0, 0, axis_index_groups=sets)
    return blocks.reshape(-1, C)


def body(features, occupancy, block_pos, kernel, out_grad):
    groups, tiles = lax.axis_size("group"), lax.axis_size("tile")
    core = (lax.axis_index("tile") & 1).astype(jnp.int32).reshape(1)
    own_in, own_grad, mask, tag, xlo, xhi, ylo, yhi = prep(block_pos, occupancy, features, out_grad)
    from_low = shifted(xhi, groups, tiles, 1, 0)
    y_from = (shifted(yhi, groups, tiles, 0, 1), shifted(ylo, groups, tiles, 0, -1))
    weights = kernel.reshape(KV * C, C)
    turned, done = turn(weights, yhi)
    scale = 1.0 / math.sqrt(groups * tiles * BLK_DEV * VOX)

    def convolved(field, slot, before, *after):
        return conv(
            field, slot, tag, (own_in, own_grad)[field], mask, (weights, turned)[field], halo, before, after
        )

    x_from = (from_low, shifted(xlo, groups, tiles, -1, 0))
    clo, chi = edges(*x_from)
    c_from = (shifted(chi, groups, tiles, 0, 1), shifted(clo, groups, tiles, 0, -1))
    halo = (*x_from, *y_from, *c_from)
    keep, send = wgrad(scale, tag, core, own_in, own_grad, (from_low, *y_from), done, clo)
    got = across(send, CORE)
    value, = small(sum_halves_kernel, [16 * CODED], [keep, got])
    value, = small(sum_blocks_kernel, [4 * CODED], [exchange(value, AXES, XY_SETS)], c_from)
    value, = small(sum_blocks_kernel, [CODED], [exchange(value, "tile", Z_LO_SETS)])
    got = across(value, Z_HI_BITS[0])
    conv_out, done = convolved(0, 0, None, value)
    conv_out, done = convolved(0, 1, conv_out, done)
    value, = small(sum_blocks_kernel, [CODED], [value, got], [done])
    got = across(value, Z_HI_BITS[1])
    feature_grad, done = convolved(1, 0, None, value)
    value, = small(sum_blocks_kernel, [16 * CODED], [value, got], [done])
    value = exchange(value, AXES, XY_SETS)
    got = across(value, CORE)
    feature_grad, done = convolved(1, 1, feature_grad, value)
    total = place(core, value, got, done)
    return (conv_out, feature_grad, total.reshape(KV, C, C))


def solution(mesh):
    in_specs = (
        P(AXES, None, None),
        P(AXES, None),
        P(AXES),
        P(),
        P(AXES, None, None),
    )
    out_specs = (P(AXES, None, None), P(AXES, None, None), P())
    return jax.shard_map(body, mesh=mesh, in_specs=in_specs, out_specs=out_specs, check_vma=False)
```

```python
import math

import jax
import jax.numpy as jnp
from jax import lax
from jax.experimental import pallas as pl
from jax.experimental.pallas import tpu as pltpu
from jax.sharding import PartitionSpec as P

BE = 8
VOX = 512
C = 128
KV = 27
BLK_DEV = 2
WIN = BE + 2
SLAB = WIN * BE * BE
SIDE = 9 * C
AXES = ("group", "tile")
FACE = 2 * BLK_DEV * BE * BE
EDGE = 2 * BLK_DEV * BE
TAG = 16
CHUNK = 108
CODED = 112
STEPS = 32000.0
HALF = 16 * CHUNK
SPARE = 8
CORE = 1
XY_SETS = [
    [(y * 4 + z_hi) * 32 + z_lo * 8 + x * 2 + core for y in range(4) for x in range(4)]
    for z_hi in range(4) for z_lo in range(4) for core in range(2)
]
Z_LO_SETS = [[z * 8 + x * 2 + core for z in range(4)] for x in range(4) for core in range(2)]
Z_HI_BITS = (32, 96)


def prep_kernel(*refs):
    sources, outs, held, sems = refs[:4], refs[4:12], refs[12:16], refs[16]
    in_ref, g_ref, mask_ref, tag_ref, xlo_ref, xhi_ref, ylo_ref, yhi_ref = outs
    copies = [pltpu.make_async_copy(src, dst, sems.at[i]) for i, (src, dst) in enumerate(zip(sources, held))]
    for copy in copies:
        copy.start()
    for copy in copies:
        copy.wait()
    pos_ref, occ_ref, feat_ref, grad_ref = held
    occ = occ_ref[...].astype(jnp.float32)
    layer = BE * BE
    tag = jnp.concatenate(
        [jnp.full((BE, C), pos_ref[s].astype(jnp.float32), jnp.float32) for s in range(BLK_DEV)]
    ).astype(jnp.bfloat16)
    tag_ref[...] = tag
    for face in (xlo_ref, xhi_ref, ylo_ref, yhi_ref):
        face[FACE:FACE + TAG, :] = tag
    for s in range(BLK_DEV):
        live = (pos_ref[s] >= 0).astype(jnp.float32)
        mask = jnp.concatenate([
            jnp.broadcast_to(occ[s:s + 1, r * C:(r + 1) * C] * live, (C, C)).T for r in range(VOX // C)
        ])
        mask_ref[s * VOX:(s + 1) * VOX, :] = mask.astype(jnp.bfloat16)
        for field, (src, dst) in enumerate(((feat_ref, in_ref), (grad_ref, g_ref))):
            value = jnp.where(mask > 0, src[s].astype(jnp.float32), 0.0)
            cube = value.reshape(BE, BE, BE, C)
            dst[s * VOX:(s + 1) * VOX, :] = value.astype(jnp.bfloat16)
            at = (field * BLK_DEV + s) * layer
            for face, piece in (
                (xlo_ref, cube[0]), (xhi_ref, cube[BE - 1]), (ylo_ref, cube[:, 0]), (yhi_ref, cube[:, BE - 1])
            ):
                face[at:at + layer, :] = piece.reshape(layer, C).astype(jnp.bfloat16)


def edges_kernel(low_ref, high_ref, ylo_ref, yhi_ref):
    layer = BE * BE
    for side, ref in enumerate((low_ref, high_ref)):
        faces = [ref[n * layer:(n + 1) * layer, :].astype(jnp.float32) for n in range(2 * BLK_DEV)]
        for y, out in ((0, ylo_ref), (BE - 1, yhi_ref)):
            edge = [face[y * BE:(y + 1) * BE] for face in faces]
            out[side * EDGE:(side + 1) * EDGE, :] = jnp.concatenate(edge).astype(jnp.bfloat16)
            at = 2 * EDGE + side * TAG
            out[at:at + TAG, :] = ref[FACE:FACE + TAG, :]


def tags_of(ref, at):
    tag = ref[at:at + TAG, :].astype(jnp.float32)
    return [tag[0:BE], tag[BE:2 * BE]]


def face_of(ref, field, shape):
    first = field * BLK_DEV
    return [
        ref[n * BE * BE:(n + 1) * BE * BE, :].astype(jnp.float32).reshape(shape)
        for n in range(first, first + BLK_DEV)
    ]


def picked(data, their_tags, here, o3):
    row = lax.broadcasted_iota(jnp.int32, (BE, C), 0)
    value = jnp.zeros((), jnp.float32)
    for n in (1, 0):
        if o3 == 0:
            wanted, moved = jnp.where(row == 0, -1.0, 0.0), pltpu.roll(data[n], 1, 1)
        elif o3 == 2:
            wanted, moved = jnp.where(row == BE - 1, 1.0, 0.0), pltpu.roll(data[n], BE - 1, 1)
        else:
            wanted, moved = jnp.zeros((BE, C), jnp.float32), data[n]
        value = jnp.where(((their_tags[n] - here) == wanted)[None], moved, value)
    return value


def fill_windows(field, slots, tag_ref, own_ref, x_from, y_from, c_from, z_ref, a_ref):
    regions = []
    own = [own_ref[n * VOX:(n + 1) * VOX, :].astype(jnp.float32).reshape(BE, BE, BE, C) for n in range(BLK_DEV)]
    own_tags = tags_of(tag_ref, 0)
    inside = slice(1, BE + 1)
    ends = (slice(0, 1), slice(WIN - 1, WIN))
    regions.append((inside, inside, own, own_tags))
    for ref, end in zip(x_from, ends):
        if ref is None:
            z_ref[:, end, inside] = jnp.zeros((3, 1, BE, BE, C), jnp.float32)
            continue
        regions.append((end, inside, face_of(ref, field, (1, BE, BE, C)), tags_of(ref, FACE)))
    for ref, end in zip(y_from, ends):
        regions.append((inside, end, face_of(ref, field, (BE, 1, BE, C)), tags_of(ref, FACE)))
    for ref, end in zip(c_from, ends):
        for side, other in enumerate(ends):
            edge = ref[side * EDGE:(side + 1) * EDGE, :].astype(jnp.float32)
            first = field * BLK_DEV
            data = [edge[n * BE:(n + 1) * BE].reshape(1, 1, BE, C) for n in range(first, first + BLK_DEV)]
            regions.append((other, end, data, tags_of(ref, 2 * EDGE + side * TAG)))
    if not c_from:
        for x in ends:
            for y in ends:
                z_ref[:, x, y] = jnp.zeros((3, 1, 1, BE, C), jnp.float32)

    for i, s in enumerate(slots):
        here = own_tags[s]
        for xs, ys, data, their_tags in regions:
            flat = [v.reshape(-1, BE, C) for v in data]
            for o3 in range(3):
                z_ref[o3, xs, ys] = picked(flat, their_tags, here, o3).reshape(data[0].shape)
        for o2 in range(3):
            for o3 in range(3):
                j = o2 * 3 + o3
                piece = z_ref[o3, :, o2:o2 + BE].reshape(SLAB, C)
                a_ref[i, :, j * C:(j + 1) * C] = piece.astype(jnp.bfloat16)


def lower_pairs(tag_ref, g_ref, x_low, y_low, y_high):
    last = BE - 1
    blank = jnp.zeros((1, BE, C), jnp.float32)

    def column(ref, field, end):
        return [v[:, end] for v in face_of(ref, field, (1, BE, BE, C))]

    inputs, rows = {0: [], 2: []}, {0: [], 2: []}
    own_tags = tags_of(tag_ref, 0)
    plane = [
        g_ref[n * VOX:n * VOX + BE * BE, :].astype(jnp.float32).reshape(BE, BE, C) for n in range(BLK_DEV)
    ]
    inputs[2] += face_of(x_low, 0, (BE * BE, C))
    for here in tags_of(x_low, FACE):
        lanes = []
        above = [
            jnp.concatenate([blank, picked(plane, own_tags, here, e3), blank]) for e3 in range(3)
        ]
        for e2 in range(3):
            lanes += [above[e3][e2:e2 + BE].reshape(BE * BE, C) for e3 in range(3)]
        rows[2].append(jnp.concatenate(lanes, axis=1))
    plans = (
        (2, 2, (x_low, last), (y_high, 0)),
        (2, 0, (x_low, 0), (y_low, 0)),
        (0, 0, (y_high, 0), (x_low, last)),
        (0, 2, (y_low, 0), (x_low, 0)),
    )
    for e1, e2, (near, near_end), (far, far_end) in plans:
        inputs[e1] += [v.reshape(BE, C) for v in column(near, 0, near_end)]
        data, their_tags = column(far, 1, far_end), tags_of(far, FACE)
        for here in tags_of(near, FACE):
            lanes = [blank.reshape(BE, C)] * 9
            for e3 in range(3):
                lanes[3 * e2 + e3] = picked(data, their_tags, here, e3).reshape(BE, C)
            rows[e1].append(jnp.concatenate(lanes, axis=1))
    result = {}
    for e1 in inputs:
        lhs, rhs = jnp.concatenate(inputs[e1]), jnp.concatenate(rows[e1])
        more = -lhs.shape[0] % C
        lhs = jnp.concatenate([lhs, jnp.zeros((more, C), jnp.float32)])
        rhs = jnp.concatenate([rhs, jnp.zeros((more, SIDE), jnp.float32)])
        result[e1] = (lhs.T.astype(jnp.bfloat16), rhs.astype(jnp.bfloat16))
    return result


def wgrad_kernel(scale, tag_ref, core_ref, in_ref, g_ref, *refs):
    halo, keep_ref, send_ref, z_ref, a_ref, total_ref = refs[:3], *refs[-5:]
    fill_windows(1, (0, 1), tag_ref, g_ref, (halo[0], None), halo[1:3], (), z_ref, a_ref)
    pairs = lower_pairs(tag_ref, g_ref, *halo)
    inner = [
        jnp.transpose(in_ref[s * VOX:(s + 1) * VOX, :].astype(jnp.float32)).astype(jnp.bfloat16)
        for s in range(BLK_DEV)
    ]
    total_ref[KV * C:, :] = jnp.zeros((SPARE, C), jnp.float32)
    for e1 in range(3):
        rows = slice(e1 * BE * BE, e1 * BE * BE + VOX)
        total = jnp.dot(inner[0], a_ref[0, rows, :], preferred_element_type=jnp.float32)
        total = total + jnp.dot(inner[1], a_ref[1, rows, :], preferred_element_type=jnp.float32)
        if e1 in pairs:
            total = total + jnp.dot(*pairs[e1], preferred_element_type=jnp.float32)
        total = total * scale
        for j in range(9):
            k = KV - 1 - (9 * e1 + j)
            total_ref[k * C:(k + 1) * C, :] = total[:, j * C:(j + 1) * C]
    core = core_ref[0]
    keep_ref[...] = total_ref[pl.ds(pl.multiple_of(core * HALF, HALF), HALF + SPARE), :]
    send_ref[...] = total_ref[pl.ds(pl.multiple_of((1 - core) * HALF, HALF), HALF + SPARE), :]


def coded(value):
    inside = lax.broadcasted_iota(jnp.int32, (CODED, C), 0) < CHUNK
    size = jnp.where(inside, jnp.abs(value), 0.0)
    exponent = jnp.floor(jnp.log2(jnp.maximum(jnp.max(size, axis=0, keepdims=True), 2.0 ** -120))) + 1.0
    steps = jnp.floor(value * (jnp.exp2(-exponent) * STEPS) + 0.5)
    return jnp.where(inside, steps, exponent).astype(jnp.int32).astype(jnp.int16)


def decoded(ref, block=0):
    code = ref[block * CODED:(block + 1) * CODED, :].astype(jnp.int32).astype(jnp.float32)
    return code * (jnp.exp2(code[CHUNK:CHUNK + 1]) * (1.0 / STEPS))


def place_kernel(core_ref, near_ref, far_ref, after_ref, out_ref):
    first = core_ref[0] == 0
    for block in range(16):
        near, far = decoded(near_ref, block)[:CHUNK], decoded(far_ref, block)[:CHUNK]
        at = block * CHUNK
        out_ref[at:at + CHUNK, :] = jnp.where(first, near, far)
        out_ref[HALF + at:HALF + at + CHUNK, :] = jnp.where(first, far, near)


def turn_kernel(w_ref, out_ref, done_ref):
    for k in range(KV):
        at = (KV - 1 - k) * C
        out_ref[at:at + C, :] = jnp.transpose(w_ref[k * C:(k + 1) * C, :].astype(jnp.float32)).astype(jnp.bfloat16)
    done_ref[...] = jnp.zeros_like(done_ref)


def conv_kernel(field, slot, tag_ref, own_ref, mask_ref, w_ref, *refs):
    halo, out_ref, done_ref, z_ref, a_ref = refs[:6], *refs[-4:]
    fill_windows(field, (slot,), tag_ref, own_ref, halo[0:2], halo[2:4], halo[4:6], z_ref, a_ref)
    total = None
    for e1 in range(3):
        rows = slice(e1 * BE * BE, e1 * BE * BE + VOX)
        part = jnp.dot(
            a_ref[0, rows, :], w_ref[e1 * SIDE:(e1 + 1) * SIDE, :], preferred_element_type=jnp.float32
        )
        total = part if total is None else total + part
    mask = mask_ref[slot * VOX:(slot + 1) * VOX, :].astype(jnp.float32)
    out_ref[0] = jnp.where(mask > 0, total, 0.0).astype(jnp.bfloat16)
    done_ref[...] = jnp.zeros_like(done_ref)


VMEM = pl.BlockSpec(memory_space=pltpu.VMEM)
ANY = pl.BlockSpec(memory_space=pl.ANY)
SMEM = pl.BlockSpec(memory_space=pltpu.SMEM)
PARAMS = pltpu.CompilerParams(vmem_limit_bytes=40 * 1024 * 1024)


def bf16(*shape):
    return jax.ShapeDtypeStruct(shape, jnp.bfloat16)


def prep(block_pos, occupancy, features, out_grad):
    field = pltpu.VMEM((BLK_DEV, VOX, C), jnp.bfloat16)
    return pl.pallas_call(
        prep_kernel,
        out_shape=[bf16(BLK_DEV * VOX, C)] * 3 + [bf16(TAG, C)] + [bf16(FACE + TAG, C)] * 4,
        in_specs=[pl.BlockSpec(memory_space=pltpu.HBM)] * 4,
        out_specs=[VMEM] * 8,
        scratch_shapes=[
            pltpu.SMEM((BLK_DEV,), jnp.int32),
            pltpu.VMEM((BLK_DEV, VOX), jnp.int32),
            field,
            field,
            pltpu.SemaphoreType.DMA((4,)),
        ],
        compiler_params=PARAMS,
        name="mask_and_faces",
    )(*[pltpu.with_memory_space_constraint(v, pltpu.HBM) for v in (block_pos, occupancy, features, out_grad)])


def edges(low, high):
    return pl.pallas_call(
        edges_kernel,
        out_shape=[bf16(2 * EDGE + 2 * TAG, C)] * 2,
        in_specs=[VMEM] * 2,
        out_specs=[VMEM] * 2,
        compiler_params=PARAMS,
        name="edges",
    )(low, high)


def turn(weights, after):
    def kernel(w_ref, after_ref, *refs):
        turn_kernel(w_ref, *refs)

    return pl.pallas_call(
        kernel,
        out_shape=[bf16(KV * C, C), jax.ShapeDtypeStruct((BE, C), jnp.float32)],
        in_specs=[VMEM, ANY],
        out_specs=[VMEM] * 2,
        compiler_params=PARAMS,
        name="turn_weights",
    )(weights, after)


def scratch(slots):
    return [
        pltpu.VMEM((3, WIN, WIN, BE, C), jnp.float32),
        pltpu.VMEM((slots, SLAB, SIDE), jnp.bfloat16),
    ]


def wgrad(scale, tag, core, own_in, own_grad, halo, *after):
    def kernel(*refs):
        wgrad_kernel(scale, *refs)

    half = jax.ShapeDtypeStruct((HALF + SPARE, C), jnp.float32)
    return pl.pallas_call(
        kernel,
        out_shape=[half, half],
        in_specs=[VMEM, SMEM] + [VMEM] * 5 + [ANY] * len(after),
        out_specs=[VMEM] * 2,
        scratch_shapes=scratch(BLK_DEV) + [pltpu.VMEM((KV * C + SPARE, C), jnp.float32)],
        compiler_params=PARAMS,
        name="kernel_gradient",
    )(tag, core, own_in, own_grad, *halo, *after)


def place(core, near, far, after):
    return pl.pallas_call(
        place_kernel,
        out_shape=jax.ShapeDtypeStruct((KV * C, C), jnp.float32),
        in_specs=[SMEM] + [VMEM] * 2 + [ANY],
        out_specs=VMEM,
        compiler_params=PARAMS,
        name="place_halves",
    )(core, near, far, after)


def conv(field, slot, tag, own, mask, weights, halo, before, after):
    def kernel(*refs):
        conv_kernel(field, slot, *refs)

    flops = 2 * KV * VOX * C * C
    args = (tag, own, mask, weights, *halo)
    extra = ([] if before is None else [before]) + list(after)
    return pl.pallas_call(
        kernel,
        grid=(1,),
        out_shape=[bf16(BLK_DEV, VOX, C), jax.ShapeDtypeStruct((BE, C), jnp.float32)],
        in_specs=[VMEM] * len(args) + [ANY] * len(extra),
        out_specs=[pl.BlockSpec((1, VOX, C), lambda i: (slot, 0, 0)), VMEM],
        scratch_shapes=scratch(1),
        input_output_aliases={} if before is None else {len(args): 0},
        compiler_params=PARAMS,
        cost_estimate=pl.CostEstimate(flops=4 * flops, bytes_accessed=2_000_000, transcendentals=0),
        name=("convolution", "feature_gradient")[field],
    )(*args, *extra)


def small(kernel, outs, args, after=()):
    after = [v for v in after if v is not None]

    def inner(*refs):
        kernel(*refs[:len(args)], *refs[len(args) + len(after):])

    many = [jax.ShapeDtypeStruct((rows, C), jnp.int16) for rows in outs]
    return pl.pallas_call(
        inner,
        out_shape=many,
        in_specs=[VMEM] * len(args) + [ANY] * len(after),
        out_specs=[VMEM] * len(many),
        compiler_params=PARAMS,
        name=kernel.__name__.removesuffix("_kernel"),
    )(*args, *after)


def sum_halves_kernel(a_ref, b_ref, out_ref):
    for block in range(HALF // CHUNK):
        rows = slice(block * CHUNK, block * CHUNK + CODED)
        out_ref[block * CODED:(block + 1) * CODED, :] = coded(a_ref[rows, :] + b_ref[rows, :])


def sum_blocks_kernel(*refs):
    *in_refs, out_ref = refs
    b = [decoded(ref, block) for ref in in_refs for block in range(ref.shape[0] // CODED)]
    while len(b) > 1:
        b = [b[i] + b[i + 1] for i in range(0, len(b), 2)]
    code = coded(b[0])
    for copy in range(out_ref.shape[0] // CODED):
        out_ref[copy * CODED:(copy + 1) * CODED, :] = code


def shifted(value, groups, tiles, up_g, up_t):
    pairs = [
        (g * tiles + t, (g + up_g) * tiles + t + up_t)
        for g in range(groups)
        for t in range(tiles)
        if 0 <= g + up_g < groups and 0 <= t + up_t < tiles
    ]
    return lax.ppermute(value, AXES, pairs)


def across(value, mask):
    count = lax.axis_size("group") * lax.axis_size("tile")
    return lax.ppermute(value, AXES, [(i, i ^ mask) for i in range(count)])


def exchange(value, axis, sets):
    count = len(sets[0])
    blocks = lax.all_to_all(value.reshape(count, -1, C), axis, 0, 0, axis_index_groups=sets)
    return blocks.reshape(-1, C)


def body(features, occupancy, block_pos, kernel, out_grad):
    groups, tiles = lax.axis_size("group"), lax.axis_size("tile")
    core = (lax.axis_index("tile") & 1).astype(jnp.int32).reshape(1)
    own_in, own_grad, mask, tag, xlo, xhi, ylo, yhi = prep(block_pos, occupancy, features, out_grad)
    from_low = shifted(xhi, groups, tiles, 1, 0)
    y_from = (shifted(yhi, groups, tiles, 0, 1), shifted(ylo, groups, tiles, 0, -1))
    weights = kernel.reshape(KV * C, C)
    turned, done = turn(weights, yhi)
    scale = 1.0 / math.sqrt(groups * tiles * BLK_DEV * VOX)

    def convolved(field, slot, before, *after):
        return conv(
            field, slot, tag, (own_in, own_grad)[field], mask, (weights, turned)[field], halo, before, after
        )

    x_from = (from_low, shifted(xlo, groups, tiles, -1, 0))
    clo, chi = edges(*x_from)
    c_from = (shifted(chi, groups, tiles, 0, 1), shifted(clo, groups, tiles, 0, -1))
    halo = (*x_from, *y_from, *c_from)
    keep, send = wgrad(scale, tag, core, own_in, own_grad, (from_low, *y_from), done, clo)
    got = across(send, CORE)
    value, = small(sum_halves_kernel, [16 * CODED], [keep, got])
    value, = small(sum_blocks_kernel, [4 * CODED], [exchange(value, AXES, XY_SETS)], c_from)
    value, = small(sum_blocks_kernel, [CODED], [exchange(value, "tile", Z_LO_SETS)])
    got = across(value, Z_HI_BITS[0])
    conv_out, done = convolved(0, 0, None, value)
    conv_out, done = convolved(0, 1, conv_out, done)
    value, = small(sum_blocks_kernel, [CODED], [value, got], [done])
    got = across(value, Z_HI_BITS[1])
    feature_grad, done = convolved(1, 0, None, value)
    value, = small(sum_blocks_kernel, [16 * CODED], [value, got], [done])
    value = exchange(value, AXES, XY_SETS)
    got = across(value, CORE)
    feature_grad, done = convolved(1, 1, feature_grad, value)
    total = place(core, value, got, done)
    return (conv_out, feature_grad, total.reshape(KV, C, C))


def solution(mesh):
    in_specs = (
        P(AXES, None, None),
        P(AXES, None),
        P(AXES),
        P(),
        P(AXES, None, None),
    )
    out_specs = (P(AXES, None, None), P(AXES, None, None), P())
    return jax.shard_map(body, mesh=mesh, in_specs=in_specs, out_specs=out_specs, check_vma=False)
```

```python
import math

import jax
import jax.numpy as jnp
from jax import lax
from jax.experimental import pallas as pl
from jax.experimental.pallas import tpu as pltpu
from jax.sharding import PartitionSpec as P

BE = 8
VOX = 512
C = 128
KV = 27
BLK_DEV = 2
WIN = BE + 2
SLAB = WIN * BE * BE
SIDE = 9 * C
AXES = ("group", "tile")
FACE = 2 * BLK_DEV * BE * BE
EDGE = 2 * BLK_DEV * BE
TAG = 16
CHUNK = 108
CODED = 112
STEPS = 32000.0
HALF = 16 * CHUNK
SPARE = 8
CORE = 1
XY_SETS = [
    [(y * 4 + z_hi) * 32 + z_lo * 8 + x * 2 + core for y in range(4) for x in range(4)]
    for z_hi in range(4) for z_lo in range(4) for core in range(2)
]
Z_LO_SETS = [[z * 8 + x * 2 + core for z in range(4)] for x in range(4) for core in range(2)]
Z_HI_BITS = (32, 96)


def prep_kernel(*refs):
    sources, outs, held, sems = refs[:4], refs[4:12], refs[12:16], refs[16]
    in_ref, g_ref, mask_ref, tag_ref, xlo_ref, xhi_ref, ylo_ref, yhi_ref = outs
    copies = [pltpu.make_async_copy(src, dst, sems.at[i]) for i, (src, dst) in enumerate(zip(sources, held))]
    for copy in copies:
        copy.start()
    for copy in copies:
        copy.wait()
    pos_ref, occ_ref, feat_ref, grad_ref = held
    occ = occ_ref[...].astype(jnp.float32)
    layer = BE * BE
    tag = jnp.concatenate(
        [jnp.full((BE, C), pos_ref[s].astype(jnp.float32), jnp.float32) for s in range(BLK_DEV)]
    ).astype(jnp.bfloat16)
    tag_ref[...] = tag
    for face in (xlo_ref, xhi_ref, ylo_ref, yhi_ref):
        face[FACE:FACE + TAG, :] = tag
    for s in range(BLK_DEV):
        live = (pos_ref[s] >= 0).astype(jnp.float32)
        mask = jnp.concatenate([
            jnp.broadcast_to(occ[s:s + 1, r * C:(r + 1) * C] * live, (C, C)).T for r in range(VOX // C)
        ])
        mask_ref[s * VOX:(s + 1) * VOX, :] = mask.astype(jnp.bfloat16)
        for field, (src, dst) in enumerate(((feat_ref, in_ref), (grad_ref, g_ref))):
            value = jnp.where(mask > 0, src[s].astype(jnp.float32), 0.0)
            cube = value.reshape(BE, BE, BE, C)
            dst[s * VOX:(s + 1) * VOX, :] = value.astype(jnp.bfloat16)
            at = (field * BLK_DEV + s) * layer
            for face, piece in (
                (xlo_ref, cube[0]), (xhi_ref, cube[BE - 1]), (ylo_ref, cube[:, 0]), (yhi_ref, cube[:, BE - 1])
            ):
                face[at:at + layer, :] = piece.reshape(layer, C).astype(jnp.bfloat16)


def edges_kernel(low_ref, high_ref, ylo_ref, yhi_ref):
    layer = BE * BE
    for side, ref in enumerate((low_ref, high_ref)):
        faces = [ref[n * layer:(n + 1) * layer, :].astype(jnp.float32) for n in range(2 * BLK_DEV)]
        for y, out in ((0, ylo_ref), (BE - 1, yhi_ref)):
            edge = [face[y * BE:(y + 1) * BE] for face in faces]
            out[side * EDGE:(side + 1) * EDGE, :] = jnp.concatenate(edge).astype(jnp.bfloat16)
            at = 2 * EDGE + side * TAG
            out[at:at + TAG, :] = ref[FACE:FACE + TAG, :]


def tags_of(ref, at):
    tag = ref[at:at + TAG, :].astype(jnp.float32)
    return [tag[0:BE], tag[BE:2 * BE]]


def face_of(ref, field, shape):
    first = field * BLK_DEV
    return [
        ref[n * BE * BE:(n + 1) * BE * BE, :].astype(jnp.float32).reshape(shape)
        for n in range(first, first + BLK_DEV)
    ]


def picked(data, their_tags, here, o3):
    row = lax.broadcasted_iota(jnp.int32, (BE, C), 0)
    value = jnp.zeros((), jnp.float32)
    for n in (1, 0):
        if o3 == 0:
            wanted, moved = jnp.where(row == 0, -1.0, 0.0), pltpu.roll(data[n], 1, 1)
        elif o3 == 2:
            wanted, moved = jnp.where(row == BE - 1, 1.0, 0.0), pltpu.roll(data[n], BE - 1, 1)
        else:
            wanted, moved = jnp.zeros((BE, C), jnp.float32), data[n]
        value = jnp.where(((their_tags[n] - here) == wanted)[None], moved, value)
    return value


def fill_windows(field, slots, tag_ref, own_ref, x_from, y_from, c_from, z_ref, a_ref):
    regions = []
    own = [own_ref[n * VOX:(n + 1) * VOX, :].astype(jnp.float32).reshape(BE, BE, BE, C) for n in range(BLK_DEV)]
    own_tags = tags_of(tag_ref, 0)
    inside = slice(1, BE + 1)
    ends = (slice(0, 1), slice(WIN - 1, WIN))
    regions.append((inside, inside, own, own_tags))
    for ref, end in zip(x_from, ends):
        if ref is None:
            z_ref[:, end, inside] = jnp.zeros((3, 1, BE, BE, C), jnp.float32)
            continue
        regions.append((end, inside, face_of(ref, field, (1, BE, BE, C)), tags_of(ref, FACE)))
    for ref, end in zip(y_from, ends):
        regions.append((inside, end, face_of(ref, field, (BE, 1, BE, C)), tags_of(ref, FACE)))
    for ref, end in zip(c_from, ends):
        for side, other in enumerate(ends):
            edge = ref[side * EDGE:(side + 1) * EDGE, :].astype(jnp.float32)
            first = field * BLK_DEV
            data = [edge[n * BE:(n + 1) * BE].reshape(1, 1, BE, C) for n in range(first, first + BLK_DEV)]
            regions.append((other, end, data, tags_of(ref, 2 * EDGE + side * TAG)))
    if not c_from:
        for x in ends:
            for y in ends:
                z_ref[:, x, y] = jnp.zeros((3, 1, 1, BE, C), jnp.float32)

    for i, s in enumerate(slots):
        here = own_tags[s]
        for xs, ys, data, their_tags in regions:
            flat = [v.reshape(-1, BE, C) for v in data]
            for o3 in range(3):
                z_ref[o3, xs, ys] = picked(flat, their_tags, here, o3).reshape(data[0].shape)
        for o2 in range(3):
            for o3 in range(3):
                j = o2 * 3 + o3
                piece = z_ref[o3, :, o2:o2 + BE].reshape(SLAB, C)
                a_ref[i, :, j * C:(j + 1) * C] = piece.astype(jnp.bfloat16)


def lower_pairs(tag_ref, g_ref, x_low, y_low, y_high):
    last = BE - 1
    blank = jnp.zeros((1, BE, C), jnp.float32)

    def column(ref, field, end):
        return [v[:, end] for v in face_of(ref, field, (1, BE, BE, C))]

    inputs, rows = {0: [], 2: []}, {0: [], 2: []}
    own_tags = tags_of(tag_ref, 0)
    plane = [
        g_ref[n * VOX:n * VOX + BE * BE, :].astype(jnp.float32).reshape(BE, BE, C) for n in range(BLK_DEV)
    ]
    inputs[2] += face_of(x_low, 0, (BE * BE, C))
    for here in tags_of(x_low, FACE):
        lanes = []
        above = [
            jnp.concatenate([blank, picked(plane, own_tags, here, e3), blank]) for e3 in range(3)
        ]
        for e2 in range(3):
            lanes += [above[e3][e2:e2 + BE].reshape(BE * BE, C) for e3 in range(3)]
        rows[2].append(jnp.concatenate(lanes, axis=1))
    plans = (
        (2, 2, (x_low, last), (y_high, 0)),
        (2, 0, (x_low, 0), (y_low, 0)),
        (0, 0, (y_high, 0), (x_low, last)),
        (0, 2, (y_low, 0), (x_low, 0)),
    )
    for e1, e2, (near, near_end), (far, far_end) in plans:
        inputs[e1] += [v.reshape(BE, C) for v in column(near, 0, near_end)]
        data, their_tags = column(far, 1, far_end), tags_of(far, FACE)
        for here in tags_of(near, FACE):
            lanes = [blank.reshape(BE, C)] * 9
            for e3 in range(3):
                lanes[3 * e2 + e3] = picked(data, their_tags, here, e3).reshape(BE, C)
            rows[e1].append(jnp.concatenate(lanes, axis=1))
    result = {}
    for e1 in inputs:
        lhs, rhs = jnp.concatenate(inputs[e1]), jnp.concatenate(rows[e1])
        more = -lhs.shape[0] % C
        lhs = jnp.concatenate([lhs, jnp.zeros((more, C), jnp.float32)])
        rhs = jnp.concatenate([rhs, jnp.zeros((more, SIDE), jnp.float32)])
        result[e1] = (lhs.T.astype(jnp.bfloat16), rhs.astype(jnp.bfloat16))
    return result


def wgrad_kernel(scale, tag_ref, core_ref, in_ref, g_ref, *refs):
    halo, keep_ref, send_ref, z_ref, a_ref, total_ref = refs[:3], *refs[-5:]
    fill_windows(1, (0, 1), tag_ref, g_ref, (halo[0], None), halo[1:3], (), z_ref, a_ref)
    pairs = lower_pairs(tag_ref, g_ref, *halo)
    inner = [
        jnp.transpose(in_ref[s * VOX:(s + 1) * VOX, :].astype(jnp.float32)).astype(jnp.bfloat16)
        for s in range(BLK_DEV)
    ]
    total_ref[KV * C:, :] = jnp.zeros((SPARE, C), jnp.float32)
    for e1 in range(3):
        rows = slice(e1 * BE * BE, e1 * BE * BE + VOX)
        total = jnp.dot(inner[0], a_ref[0, rows, :], preferred_element_type=jnp.float32)
        total = total + jnp.dot(inner[1], a_ref[1, rows, :], preferred_element_type=jnp.float32)
        if e1 in pairs:
            total = total + jnp.dot(*pairs[e1], preferred_element_type=jnp.float32)
        total = total * scale
        for j in range(9):
            k = KV - 1 - (9 * e1 + j)
            total_ref[k * C:(k + 1) * C, :] = total[:, j * C:(j + 1) * C]
    core = core_ref[0]
    keep_ref[...] = total_ref[pl.ds(pl.multiple_of(core * HALF, HALF), HALF + SPARE), :]
    send_ref[...] = total_ref[pl.ds(pl.multiple_of((1 - core) * HALF, HALF), HALF + SPARE), :]


def coded(value):
    inside = lax.broadcasted_iota(jnp.int32, (CODED, C), 0) < CHUNK
    size = jnp.where(inside, jnp.abs(value), 0.0)
    exponent = jnp.floor(jnp.log2(jnp.maximum(jnp.max(size, axis=0, keepdims=True), 2.0 ** -120))) + 1.0
    steps = jnp.floor(value * (jnp.exp2(-exponent) * STEPS) + 0.5)
    return jnp.where(inside, steps, exponent).astype(jnp.int32).astype(jnp.int16)


def decoded(ref, block=0):
    code = ref[block * CODED:(block + 1) * CODED, :].astype(jnp.int32).astype(jnp.float32)
    return code * (jnp.exp2(code[CHUNK:CHUNK + 1]) * (1.0 / STEPS))


def place_half_kernel(half_ref, code_ref, *refs):
    out_ref = refs[-1]
    for block in range(16):
        out_ref[block * CHUNK:(block + 1) * CHUNK, :] = decoded(code_ref, block)[:CHUNK]


def turn_kernel(w_ref, out_ref, done_ref):
    for k in range(KV):
        at = (KV - 1 - k) * C
        out_ref[at:at + C, :] = jnp.transpose(w_ref[k * C:(k + 1) * C, :].astype(jnp.float32)).astype(jnp.bfloat16)
    done_ref[...] = jnp.zeros_like(done_ref)


def conv_kernel(field, slot, tag_ref, own_ref, mask_ref, w_ref, *refs):
    halo, out_ref, done_ref, z_ref, a_ref = refs[:6], *refs[-4:]
    fill_windows(field, (slot,), tag_ref, own_ref, halo[0:2], halo[2:4], halo[4:6], z_ref, a_ref)
    total = None
    for e1 in range(3):
        rows = slice(e1 * BE * BE, e1 * BE * BE + VOX)
        part = jnp.dot(
            a_ref[0, rows, :], w_ref[e1 * SIDE:(e1 + 1) * SIDE, :], preferred_element_type=jnp.float32
        )
        total = part if total is None else total + part
    mask = mask_ref[slot * VOX:(slot + 1) * VOX, :].astype(jnp.float32)
    out_ref[0] = jnp.where(mask > 0, total, 0.0).astype(jnp.bfloat16)
    done_ref[...] = jnp.zeros_like(done_ref)


VMEM = pl.BlockSpec(memory_space=pltpu.VMEM)
ANY = pl.BlockSpec(memory_space=pl.ANY)
SMEM = pl.BlockSpec(memory_space=pltpu.SMEM)
PARAMS = pltpu.CompilerParams(vmem_limit_bytes=40 * 1024 * 1024)


def bf16(*shape):
    return jax.ShapeDtypeStruct(shape, jnp.bfloat16)


def prep(block_pos, occupancy, features, out_grad):
    field = pltpu.VMEM((BLK_DEV, VOX, C), jnp.bfloat16)
    return pl.pallas_call(
        prep_kernel,
        out_shape=[bf16(BLK_DEV * VOX, C)] * 3 + [bf16(TAG, C)] + [bf16(FACE + TAG, C)] * 4,
        in_specs=[pl.BlockSpec(memory_space=pltpu.HBM)] * 4,
        out_specs=[VMEM] * 8,
        scratch_shapes=[
            pltpu.SMEM((BLK_DEV,), jnp.int32),
            pltpu.VMEM((BLK_DEV, VOX), jnp.int32),
            field,
            field,
            pltpu.SemaphoreType.DMA((4,)),
        ],
        compiler_params=PARAMS,
        name="mask_and_faces",
    )(*[pltpu.with_memory_space_constraint(v, pltpu.HBM) for v in (block_pos, occupancy, features, out_grad)])


def edges(low, high):
    return pl.pallas_call(
        edges_kernel,
        out_shape=[bf16(2 * EDGE + 2 * TAG, C)] * 2,
        in_specs=[VMEM] * 2,
        out_specs=[VMEM] * 2,
        compiler_params=PARAMS,
        name="edges",
    )(low, high)


def passed(value, after):
    def kernel(value_ref, after_ref, out_ref):
        pass

    return pl.pallas_call(
        kernel,
        out_shape=jax.ShapeDtypeStruct(value.shape, value.dtype),
        in_specs=[ANY] * 2,
        out_specs=ANY,
        input_output_aliases={0: 0},
        compiler_params=PARAMS,
        name="passed",
    )(value, after)


def turn(weights, after):
    def kernel(w_ref, after_ref, *refs):
        turn_kernel(w_ref, *refs)

    return pl.pallas_call(
        kernel,
        out_shape=[bf16(KV * C, C), jax.ShapeDtypeStruct((BE, C), jnp.float32)],
        in_specs=[VMEM, ANY],
        out_specs=[VMEM] * 2,
        compiler_params=PARAMS,
        name="turn_weights",
    )(weights, after)


def scratch(slots):
    return [
        pltpu.VMEM((3, WIN, WIN, BE, C), jnp.float32),
        pltpu.VMEM((slots, SLAB, SIDE), jnp.bfloat16),
    ]


def wgrad(scale, tag, core, own_in, own_grad, halo, *after):
    def kernel(*refs):
        wgrad_kernel(scale, *refs)

    half = jax.ShapeDtypeStruct((HALF + SPARE, C), jnp.float32)
    return pl.pallas_call(
        kernel,
        out_shape=[half, half],
        in_specs=[VMEM, SMEM] + [VMEM] * 5 + [ANY] * len(after),
        out_specs=[VMEM] * 2,
        scratch_shapes=scratch(BLK_DEV) + [pltpu.VMEM((KV * C + SPARE, C), jnp.float32)],
        compiler_params=PARAMS,
        name="kernel_gradient",
    )(tag, core, own_in, own_grad, *halo, *after)


def place_half(half, code, before):
    extra = [] if before is None else [before]
    return pl.pallas_call(
        place_half_kernel,
        out_shape=jax.ShapeDtypeStruct((KV * C, C), jnp.float32),
        grid_spec=pltpu.PrefetchScalarGridSpec(
            num_scalar_prefetch=1,
            grid=(1,),
            in_specs=[VMEM] + [ANY] * len(extra),
            out_specs=pl.BlockSpec((HALF, C), lambda i, half: (half[0], 0)),
        ),
        input_output_aliases={} if before is None else {2: 0},
        compiler_params=PARAMS,
        name="place_half",
    )(half, code, *extra)


def conv(field, slot, tag, own, mask, weights, halo, before, after):
    def kernel(*refs):
        conv_kernel(field, slot, *refs)

    flops = 2 * KV * VOX * C * C
    args = (tag, own, mask, weights, *halo)
    extra = ([] if before is None else [before]) + list(after)
    return pl.pallas_call(
        kernel,
        grid=(1,),
        out_shape=[bf16(BLK_DEV, VOX, C), jax.ShapeDtypeStruct((BE, C), jnp.float32)],
        in_specs=[VMEM] * len(args) + [ANY] * len(extra),
        out_specs=[pl.BlockSpec((1, VOX, C), lambda i: (slot, 0, 0)), VMEM],
        scratch_shapes=scratch(1),
        input_output_aliases={} if before is None else {len(args): 0},
        compiler_params=PARAMS,
        cost_estimate=pl.CostEstimate(flops=4 * flops, bytes_accessed=2_000_000, transcendentals=0),
        name=("convolution", "feature_gradient")[field],
    )(*args, *extra)


def small(kernel, outs, args, after=()):
    after = [v for v in after if v is not None]

    def inner(*refs):
        kernel(*refs[:len(args)], *refs[len(args) + len(after):])

    many = [jax.ShapeDtypeStruct((rows, C), jnp.int16) for rows in outs]
    return pl.pallas_call(
        inner,
        out_shape=many,
        in_specs=[VMEM] * len(args) + [ANY] * len(after),
        out_specs=[VMEM] * len(many),
        compiler_params=PARAMS,
        name=kernel.__name__.removesuffix("_kernel"),
    )(*args, *after)


def sum_halves_kernel(a_ref, b_ref, out_ref):
    for block in range(HALF // CHUNK):
        rows = slice(block * CHUNK, block * CHUNK + CODED)
        out_ref[block * CODED:(block + 1) * CODED, :] = coded(a_ref[rows, :] + b_ref[rows, :])


def sum_blocks_kernel(*refs):
    *in_refs, out_ref = refs
    b = [decoded(ref, block) for ref in in_refs for block in range(ref.shape[0] // CODED)]
    while len(b) > 1:
        b = [b[i] + b[i + 1] for i in range(0, len(b), 2)]
    code = coded(b[0])
    for copy in range(out_ref.shape[0] // CODED):
        out_ref[copy * CODED:(copy + 1) * CODED, :] = code


def shifted(value, groups, tiles, up_g, up_t):
    pairs = [
        (g * tiles + t, (g + up_g) * tiles + t + up_t)
        for g in range(groups)
        for t in range(tiles)
        if 0 <= g + up_g < groups and 0 <= t + up_t < tiles
    ]
    return lax.ppermute(value, AXES, pairs)


def across(value, mask):
    count = lax.axis_size("group") * lax.axis_size("tile")
    return lax.ppermute(value, AXES, [(i, i ^ mask) for i in range(count)])


def exchange(value, axis, sets):
    count = len(sets[0])
    blocks = lax.all_to_all(value.reshape(count, -1, C), axis, 0, 0, axis_index_groups=sets)
    return blocks.reshape(-1, C)


def body(features, occupancy, block_pos, kernel, out_grad):
    groups, tiles = lax.axis_size("group"), lax.axis_size("tile")
    core = (lax.axis_index("tile") & 1).astype(jnp.int32).reshape(1)
    own_in, own_grad, mask, tag, xlo, xhi, ylo, yhi = prep(block_pos, occupancy, features, out_grad)
    from_low = shifted(xhi, groups, tiles, 1, 0)
    y_from = (shifted(yhi, groups, tiles, 0, 1), shifted(ylo, groups, tiles, 0, -1))
    weights = kernel.reshape(KV * C, C)
    turned, done = turn(weights, yhi)
    scale = 1.0 / math.sqrt(groups * tiles * BLK_DEV * VOX)

    def convolved(field, slot, before, *after):
        return conv(
            field, slot, tag, (own_in, own_grad)[field], mask, (weights, turned)[field], halo, before, after
        )

    x_from = (from_low, shifted(xlo, groups, tiles, -1, 0))
    clo, chi = edges(*x_from)
    c_from = (shifted(chi, groups, tiles, 0, 1), shifted(clo, groups, tiles, 0, -1))
    halo = (*x_from, *y_from, *c_from)
    keep, send = wgrad(scale, tag, core, own_in, own_grad, (from_low, *y_from), done, clo)
    got = across(send, CORE)
    value, = small(sum_halves_kernel, [16 * CODED], [keep, got])
    value, = small(sum_blocks_kernel, [4 * CODED], [exchange(value, AXES, XY_SETS)], c_from)
    value, = small(sum_blocks_kernel, [CODED], [exchange(value, "tile", Z_LO_SETS)])
    got = across(value, Z_HI_BITS[0])
    conv_out, done = convolved(0, 0, None, value)
    value, = small(sum_blocks_kernel, [CODED], [value, got], [done])
    got = across(value, Z_HI_BITS[1])
    conv_out, done = convolved(0, 1, conv_out, value)
    value, = small(sum_blocks_kernel, [16 * CODED], [value, got], [done])
    feature_grad, done = convolved(1, 0, None, value)
    feature_grad, done = convolved(1, 1, feature_grad, done)
    value = passed(exchange(value, AXES, XY_SETS), done)
    got = across(value, CORE)
    total = place_half(core, value, None)
    total = place_half(1 - core, got, total)
    return (conv_out, feature_grad, total.reshape(KV, C, C))


def solution(mesh):
    in_specs = (
        P(AXES, None, None),
        P(AXES, None),
        P(AXES),
        P(),
        P(AXES, None, None),
    )
    out_specs = (P(AXES, None, None), P(AXES, None, None), P())
    return jax.shard_map(body, mesh=mesh, in_specs=in_specs, out_specs=out_specs, check_vma=False)
```

```python
import math

import jax
import jax.numpy as jnp
from jax import lax
from jax.experimental import pallas as pl
from jax.experimental.pallas import tpu as pltpu
from jax.sharding import PartitionSpec as P

BE = 8
VOX = 512
C = 128
KV = 27
BLK_DEV = 2
WIN = BE + 2
SLAB = WIN * BE * BE
SIDE = 9 * C
AXES = ("group", "tile")
FACE = 2 * BLK_DEV * BE * BE
EDGE = 2 * BLK_DEV * BE
TAG = 16
CHUNK = 108
CODED = 112
STEPS = 32000.0
HALF = 16 * CHUNK
SPARE = 8
CORE = 1
XY_SETS = [
    [(y * 4 + z_hi) * 32 + z_lo * 8 + x * 2 + core for y in range(4) for x in range(4)]
    for z_hi in range(4) for z_lo in range(4) for core in range(2)
]
Z_LO_SETS = [[z * 8 + x * 2 + core for z in range(4)] for x in range(4) for core in range(2)]
Z_HI_BITS = (32, 96)


def prep_kernel(*refs):
    sources, outs, held, sems = refs[:4], refs[4:12], refs[12:16], refs[16]
    in_ref, g_ref, mask_ref, tag_ref, xlo_ref, xhi_ref, ylo_ref, yhi_ref = outs
    copies = [pltpu.make_async_copy(src, dst, sems.at[i]) for i, (src, dst) in enumerate(zip(sources, held))]
    for copy in copies:
        copy.start()
    for copy in copies:
        copy.wait()
    pos_ref, occ_ref, feat_ref, grad_ref = held
    occ = occ_ref[...].astype(jnp.float32)
    layer = BE * BE
    tag = jnp.concatenate(
        [jnp.full((BE, C), pos_ref[s].astype(jnp.float32), jnp.float32) for s in range(BLK_DEV)]
    ).astype(jnp.bfloat16)
    tag_ref[...] = tag
    for face in (xlo_ref, xhi_ref, ylo_ref, yhi_ref):
        face[FACE:FACE + TAG, :] = tag
    for s in range(BLK_DEV):
        live = (pos_ref[s] >= 0).astype(jnp.float32)
        mask = jnp.concatenate([
            jnp.broadcast_to(occ[s:s + 1, r * C:(r + 1) * C] * live, (C, C)).T for r in range(VOX // C)
        ])
        mask_ref[s * VOX:(s + 1) * VOX, :] = mask.astype(jnp.bfloat16)
        for field, (src, dst) in enumerate(((feat_ref, in_ref), (grad_ref, g_ref))):
            value = jnp.where(mask > 0, src[s].astype(jnp.float32), 0.0)
            cube = value.reshape(BE, BE, BE, C)
            dst[s * VOX:(s + 1) * VOX, :] = value.astype(jnp.bfloat16)
            at = (field * BLK_DEV + s) * layer
            for face, piece in (
                (xlo_ref, cube[0]), (xhi_ref, cube[BE - 1]), (ylo_ref, cube[:, 0]), (yhi_ref, cube[:, BE - 1])
            ):
                face[at:at + layer, :] = piece.reshape(layer, C).astype(jnp.bfloat16)


def edges_kernel(low_ref, high_ref, ylo_ref, yhi_ref):
    layer = BE * BE
    for side, ref in enumerate((low_ref, high_ref)):
        faces = [ref[n * layer:(n + 1) * layer, :].astype(jnp.float32) for n in range(2 * BLK_DEV)]
        for y, out in ((0, ylo_ref), (BE - 1, yhi_ref)):
            edge = [face[y * BE:(y + 1) * BE] for face in faces]
            out[side * EDGE:(side + 1) * EDGE, :] = jnp.concatenate(edge).astype(jnp.bfloat16)
            at = 2 * EDGE + side * TAG
            out[at:at + TAG, :] = ref[FACE:FACE + TAG, :]


def tags_of(ref, at):
    tag = ref[at:at + TAG, :].astype(jnp.float32)
    return [tag[0:BE], tag[BE:2 * BE]]


def face_of(ref, field, shape):
    first = field * BLK_DEV
    return [
        ref[n * BE * BE:(n + 1) * BE * BE, :].astype(jnp.float32).reshape(shape)
        for n in range(first, first + BLK_DEV)
    ]


def picked(data, their_tags, here, o3):
    row = lax.broadcasted_iota(jnp.int32, (BE, C), 0)
    value = jnp.zeros((), jnp.float32)
    for n in (1, 0):
        if o3 == 0:
            wanted, moved = jnp.where(row == 0, -1.0, 0.0), pltpu.roll(data[n], 1, 1)
        elif o3 == 2:
            wanted, moved = jnp.where(row == BE - 1, 1.0, 0.0), pltpu.roll(data[n], BE - 1, 1)
        else:
            wanted, moved = jnp.zeros((BE, C), jnp.float32), data[n]
        value = jnp.where(((their_tags[n] - here) == wanted)[None], moved, value)
    return value


def fill_windows(field, slots, tag_ref, own_ref, x_from, y_from, c_from, z_ref, a_ref):
    regions = []
    own = [own_ref[n * VOX:(n + 1) * VOX, :].astype(jnp.float32).reshape(BE, BE, BE, C) for n in range(BLK_DEV)]
    own_tags = tags_of(tag_ref, 0)
    inside = slice(1, BE + 1)
    ends = (slice(0, 1), slice(WIN - 1, WIN))
    regions.append((inside, inside, own, own_tags))
    for ref, end in zip(x_from, ends):
        if ref is None:
            z_ref[:, end, inside] = jnp.zeros((3, 1, BE, BE, C), jnp.float32)
            continue
        regions.append((end, inside, face_of(ref, field, (1, BE, BE, C)), tags_of(ref, FACE)))
    for ref, end in zip(y_from, ends):
        regions.append((inside, end, face_of(ref, field, (BE, 1, BE, C)), tags_of(ref, FACE)))
    for ref, end in zip(c_from, ends):
        for side, other in enumerate(ends):
            edge = ref[side * EDGE:(side + 1) * EDGE, :].astype(jnp.float32)
            first = field * BLK_DEV
            data = [edge[n * BE:(n + 1) * BE].reshape(1, 1, BE, C) for n in range(first, first + BLK_DEV)]
            regions.append((other, end, data, tags_of(ref, 2 * EDGE + side * TAG)))
    if not c_from:
        for x in ends:
            for y in ends:
                z_ref[:, x, y] = jnp.zeros((3, 1, 1, BE, C), jnp.float32)

    for i, s in enumerate(slots):
        here = own_tags[s]
        for xs, ys, data, their_tags in regions:
            flat = [v.reshape(-1, BE, C) for v in data]
            for o3 in range(3):
                z_ref[o3, xs, ys] = picked(flat, their_tags, here, o3).reshape(data[0].shape)
        for o2 in range(3):
            for o3 in range(3):
                j = o2 * 3 + o3
                piece = z_ref[o3, :, o2:o2 + BE].reshape(SLAB, C)
                a_ref[i, :, j * C:(j + 1) * C] = piece.astype(jnp.bfloat16)


def lower_pairs(tag_ref, g_ref, x_low, y_low, y_high):
    last = BE - 1
    blank = jnp.zeros((1, BE, C), jnp.float32)

    def column(ref, field, end):
        return [v[:, end] for v in face_of(ref, field, (1, BE, BE, C))]

    inputs, rows = {0: [], 2: []}, {0: [], 2: []}
    own_tags = tags_of(tag_ref, 0)
    plane = [
        g_ref[n * VOX:n * VOX + BE * BE, :].astype(jnp.float32).reshape(BE, BE, C) for n in range(BLK_DEV)
    ]
    inputs[2] += face_of(x_low, 0, (BE * BE, C))
    for here in tags_of(x_low, FACE):
        lanes = []
        above = [
            jnp.concatenate([blank, picked(plane, own_tags, here, e3), blank]) for e3 in range(3)
        ]
        for e2 in range(3):
            lanes += [above[e3][e2:e2 + BE].reshape(BE * BE, C) for e3 in range(3)]
        rows[2].append(jnp.concatenate(lanes, axis=1))
    plans = (
        (2, 2, (x_low, last), (y_high, 0)),
        (2, 0, (x_low, 0), (y_low, 0)),
        (0, 0, (y_high, 0), (x_low, last)),
        (0, 2, (y_low, 0), (x_low, 0)),
    )
    for e1, e2, (near, near_end), (far, far_end) in plans:
        inputs[e1] += [v.reshape(BE, C) for v in column(near, 0, near_end)]
        data, their_tags = column(far, 1, far_end), tags_of(far, FACE)
        for here in tags_of(near, FACE):
            lanes = [blank.reshape(BE, C)] * 9
            for e3 in range(3):
                lanes[3 * e2 + e3] = picked(data, their_tags, here, e3).reshape(BE, C)
            rows[e1].append(jnp.concatenate(lanes, axis=1))
    result = {}
    for e1 in inputs:
        lhs, rhs = jnp.concatenate(inputs[e1]), jnp.concatenate(rows[e1])
        more = -lhs.shape[0] % C
        lhs = jnp.concatenate([lhs, jnp.zeros((more, C), jnp.float32)])
        rhs = jnp.concatenate([rhs, jnp.zeros((more, SIDE), jnp.float32)])
        result[e1] = (lhs.T.astype(jnp.bfloat16), rhs.astype(jnp.bfloat16))
    return result


def wgrad_kernel(scale, tag_ref, core_ref, in_ref, g_ref, *refs):
    halo, keep_ref, send_ref, z_ref, a_ref, total_ref = refs[:3], *refs[-5:]
    fill_windows(1, (0, 1), tag_ref, g_ref, (halo[0], None), halo[1:3], (), z_ref, a_ref)
    pairs = lower_pairs(tag_ref, g_ref, *halo)
    inner = [
        jnp.transpose(in_ref[s * VOX:(s + 1) * VOX, :].astype(jnp.float32)).astype(jnp.bfloat16)
        for s in range(BLK_DEV)
    ]
    total_ref[KV * C:, :] = jnp.zeros((SPARE, C), jnp.float32)
    for e1 in range(3):
        rows = slice(e1 * BE * BE, e1 * BE * BE + VOX)
        total = jnp.dot(inner[0], a_ref[0, rows, :], preferred_element_type=jnp.float32)
        total = total + jnp.dot(inner[1], a_ref[1, rows, :], preferred_element_type=jnp.float32)
        if e1 in pairs:
            total = total + jnp.dot(*pairs[e1], preferred_element_type=jnp.float32)
        total = total * scale
        for j in range(9):
            k = KV - 1 - (9 * e1 + j)
            total_ref[k * C:(k + 1) * C, :] = total[:, j * C:(j + 1) * C]
    core = core_ref[0]
    keep_ref[...] = total_ref[pl.ds(pl.multiple_of(core * HALF, HALF), HALF + SPARE), :]
    for block in range(16):
        at = block * CHUNK
        other = jnp.where(
            core == 0, total_ref[HALF + at:HALF + at + CODED, :], total_ref[at:at + CODED, :]
        )
        send_ref[block * CODED:(block + 1) * CODED, :] = coded(other)


def coded(value):
    inside = lax.broadcasted_iota(jnp.int32, (CODED, C), 0) < CHUNK
    size = jnp.where(inside, jnp.abs(value), 0.0)
    exponent = jnp.floor(jnp.log2(jnp.maximum(jnp.max(size, axis=0, keepdims=True), 2.0 ** -120))) + 1.0
    steps = jnp.floor(value * (jnp.exp2(-exponent) * STEPS) + 0.5)
    return jnp.where(inside, steps, exponent).astype(jnp.int32).astype(jnp.int16)


def decoded(ref, block=0):
    code = ref[block * CODED:(block + 1) * CODED, :].astype(jnp.int32).astype(jnp.float32)
    return code * (jnp.exp2(code[CHUNK:CHUNK + 1]) * (1.0 / STEPS))


def place_half_kernel(half_ref, code_ref, *refs):
    out_ref = refs[-1]
    for block in range(16):
        out_ref[block * CHUNK:(block + 1) * CHUNK, :] = decoded(code_ref, block)[:CHUNK]


def turn_kernel(w_ref, out_ref, done_ref):
    for k in range(KV):
        at = (KV - 1 - k) * C
        out_ref[at:at + C, :] = jnp.transpose(w_ref[k * C:(k + 1) * C, :].astype(jnp.float32)).astype(jnp.bfloat16)
    done_ref[...] = jnp.zeros_like(done_ref)


def conv_kernel(field, slot, tag_ref, own_ref, mask_ref, w_ref, *refs):
    halo, out_ref, done_ref, z_ref, a_ref = refs[:6], *refs[-4:]
    fill_windows(field, (slot,), tag_ref, own_ref, halo[0:2], halo[2:4], halo[4:6], z_ref, a_ref)
    total = None
    for e1 in range(3):
        rows = slice(e1 * BE * BE, e1 * BE * BE + VOX)
        part = jnp.dot(
            a_ref[0, rows, :], w_ref[e1 * SIDE:(e1 + 1) * SIDE, :], preferred_element_type=jnp.float32
        )
        total = part if total is None else total + part
    mask = mask_ref[slot * VOX:(slot + 1) * VOX, :].astype(jnp.float32)
    out_ref[0] = jnp.where(mask > 0, total, 0.0).astype(jnp.bfloat16)
    done_ref[...] = jnp.zeros_like(done_ref)


VMEM = pl.BlockSpec(memory_space=pltpu.VMEM)
ANY = pl.BlockSpec(memory_space=pl.ANY)
SMEM = pl.BlockSpec(memory_space=pltpu.SMEM)
PARAMS = pltpu.CompilerParams(vmem_limit_bytes=40 * 1024 * 1024)


def bf16(*shape):
    return jax.ShapeDtypeStruct(shape, jnp.bfloat16)


def prep(block_pos, occupancy, features, out_grad):
    field = pltpu.VMEM((BLK_DEV, VOX, C), jnp.bfloat16)
    return pl.pallas_call(
        prep_kernel,
        out_shape=[bf16(BLK_DEV * VOX, C)] * 3 + [bf16(TAG, C)] + [bf16(FACE + TAG, C)] * 4,
        in_specs=[pl.BlockSpec(memory_space=pltpu.HBM)] * 4,
        out_specs=[VMEM] * 8,
        scratch_shapes=[
            pltpu.SMEM((BLK_DEV,), jnp.int32),
            pltpu.VMEM((BLK_DEV, VOX), jnp.int32),
            field,
            field,
            pltpu.SemaphoreType.DMA((4,)),
        ],
        compiler_params=PARAMS,
        name="mask_and_faces",
    )(*[pltpu.with_memory_space_constraint(v, pltpu.HBM) for v in (block_pos, occupancy, features, out_grad)])


def edges(low, high):
    return pl.pallas_call(
        edges_kernel,
        out_shape=[bf16(2 * EDGE + 2 * TAG, C)] * 2,
        in_specs=[VMEM] * 2,
        out_specs=[VMEM] * 2,
        compiler_params=PARAMS,
        name="edges",
    )(low, high)


def passed(value, after):
    def kernel(value_ref, after_ref, out_ref):
        pass

    return pl.pallas_call(
        kernel,
        out_shape=jax.ShapeDtypeStruct(value.shape, value.dtype),
        in_specs=[ANY] * 2,
        out_specs=ANY,
        input_output_aliases={0: 0},
        compiler_params=PARAMS,
        name="passed",
    )(value, after)


def turn(weights, after):
    def kernel(w_ref, after_ref, *refs):
        turn_kernel(w_ref, *refs)

    return pl.pallas_call(
        kernel,
        out_shape=[bf16(KV * C, C), jax.ShapeDtypeStruct((BE, C), jnp.float32)],
        in_specs=[VMEM, ANY],
        out_specs=[VMEM] * 2,
        compiler_params=PARAMS,
        name="turn_weights",
    )(weights, after)


def scratch(slots):
    return [
        pltpu.VMEM((3, WIN, WIN, BE, C), jnp.float32),
        pltpu.VMEM((slots, SLAB, SIDE), jnp.bfloat16),
    ]


def wgrad(scale, tag, core, own_in, own_grad, halo, *after):
    def kernel(*refs):
        wgrad_kernel(scale, *refs)

    half = jax.ShapeDtypeStruct((HALF + SPARE, C), jnp.float32)
    return pl.pallas_call(
        kernel,
        out_shape=[half, jax.ShapeDtypeStruct((16 * CODED, C), jnp.int16)],
        in_specs=[VMEM, SMEM] + [VMEM] * 5 + [ANY] * len(after),
        out_specs=[VMEM] * 2,
        scratch_shapes=scratch(BLK_DEV) + [pltpu.VMEM((KV * C + SPARE, C), jnp.float32)],
        compiler_params=PARAMS,
        name="kernel_gradient",
    )(tag, core, own_in, own_grad, *halo, *after)


def place_half(half, code, before):
    extra = [] if before is None else [before]
    return pl.pallas_call(
        place_half_kernel,
        out_shape=jax.ShapeDtypeStruct((KV * C, C), jnp.float32),
        grid_spec=pltpu.PrefetchScalarGridSpec(
            num_scalar_prefetch=1,
            grid=(1,),
            in_specs=[VMEM] + [ANY] * len(extra),
            out_specs=pl.BlockSpec((HALF, C), lambda i, half: (half[0], 0)),
        ),
        input_output_aliases={} if before is None else {2: 0},
        compiler_params=PARAMS,
        name="place_half",
    )(half, code, *extra)


def conv(field, slot, tag, own, mask, weights, halo, before, after):
    def kernel(*refs):
        conv_kernel(field, slot, *refs)

    flops = 2 * KV * VOX * C * C
    args = (tag, own, mask, weights, *halo)
    extra = ([] if before is None else [before]) + list(after)
    return pl.pallas_call(
        kernel,
        grid=(1,),
        out_shape=[bf16(BLK_DEV, VOX, C), jax.ShapeDtypeStruct((BE, C), jnp.float32)],
        in_specs=[VMEM] * len(args) + [ANY] * len(extra),
        out_specs=[pl.BlockSpec((1, VOX, C), lambda i: (slot, 0, 0)), VMEM],
        scratch_shapes=scratch(1),
        input_output_aliases={} if before is None else {len(args): 0},
        compiler_params=PARAMS,
        cost_estimate=pl.CostEstimate(flops=4 * flops, bytes_accessed=2_000_000, transcendentals=0),
        name=("convolution", "feature_gradient")[field],
    )(*args, *extra)


def small(kernel, outs, args, after=()):
    after = [v for v in after if v is not None]

    def inner(*refs):
        kernel(*refs[:len(args)], *refs[len(args) + len(after):])

    many = [jax.ShapeDtypeStruct((rows, C), jnp.int16) for rows in outs]
    return pl.pallas_call(
        inner,
        out_shape=many,
        in_specs=[VMEM] * len(args) + [ANY] * len(after),
        out_specs=[VMEM] * len(many),
        compiler_params=PARAMS,
        name=kernel.__name__.removesuffix("_kernel"),
    )(*args, *after)


def sum_halves_kernel(a_ref, b_ref, out_ref):
    for block in range(HALF // CHUNK):
        rows = slice(block * CHUNK, block * CHUNK + CODED)
        out_ref[block * CODED:(block + 1) * CODED, :] = coded(a_ref[rows, :] + decoded(b_ref, block))


def sum_blocks_kernel(*refs):
    *in_refs, out_ref = refs
    b = [decoded(ref, block) for ref in in_refs for block in range(ref.shape[0] // CODED)]
    while len(b) > 1:
        b = [b[i] + b[i + 1] for i in range(0, len(b), 2)]
    code = coded(b[0])
    for copy in range(out_ref.shape[0] // CODED):
        out_ref[copy * CODED:(copy + 1) * CODED, :] = code


def shifted(value, groups, tiles, up_g, up_t):
    pairs = [
        (g * tiles + t, (g + up_g) * tiles + t + up_t)
        for g in range(groups)
        for t in range(tiles)
        if 0 <= g + up_g < groups and 0 <= t + up_t < tiles
    ]
    return lax.ppermute(value, AXES, pairs)


def across(value, mask):
    count = lax.axis_size("group") * lax.axis_size("tile")
    return lax.ppermute(value, AXES, [(i, i ^ mask) for i in range(count)])


def exchange(value, axis, sets):
    count = len(sets[0])
    blocks = lax.all_to_all(value.reshape(count, -1, C), axis, 0, 0, axis_index_groups=sets)
    return blocks.reshape(-1, C)


def body(features, occupancy, block_pos, kernel, out_grad):
    groups, tiles = lax.axis_size("group"), lax.axis_size("tile")
    core = (lax.axis_index("tile") & 1).astype(jnp.int32).reshape(1)
    own_in, own_grad, mask, tag, xlo, xhi, ylo, yhi = prep(block_pos, occupancy, features, out_grad)
    from_low = shifted(xhi, groups, tiles, 1, 0)
    y_from = (shifted(yhi, groups, tiles, 0, 1), shifted(ylo, groups, tiles, 0, -1))
    weights = kernel.reshape(KV * C, C)
    turned, done = turn(weights, yhi)
    scale = 1.0 / math.sqrt(groups * tiles * BLK_DEV * VOX)

    def convolved(field, slot, before, *after):
        return conv(
            field, slot, tag, (own_in, own_grad)[field], mask, (weights, turned)[field], halo, before, after
        )

    x_from = (from_low, shifted(xlo, groups, tiles, -1, 0))
    clo, chi = edges(*x_from)
    c_from = (shifted(chi, groups, tiles, 0, 1), shifted(clo, groups, tiles, 0, -1))
    halo = (*x_from, *y_from, *c_from)
    keep, send = wgrad(scale, tag, core, own_in, own_grad, (from_low, *y_from), done, x_from[1])
    got = across(send, CORE)
    value, = small(sum_halves_kernel, [16 * CODED], [keep, got])
    value, = small(sum_blocks_kernel, [4 * CODED], [exchange(value, AXES, XY_SETS)], c_from)
    value, = small(sum_blocks_kernel, [CODED], [exchange(value, "tile", Z_LO_SETS)])
    got = across(value, Z_HI_BITS[0])
    conv_out, done = convolved(0, 0, None, value)
    value, = small(sum_blocks_kernel, [CODED], [value, got], [done])
    got = across(value, Z_HI_BITS[1])
    conv_out, done = convolved(0, 1, conv_out, value)
    value, = small(sum_blocks_kernel, [16 * CODED], [value, got], [done])
    feature_grad, done = convolved(1, 0, None, value)
    feature_grad, done = convolved(1, 1, feature_grad, done)
    value = passed(exchange(value, AXES, XY_SETS), done)
    got = across(value, CORE)
    total = place_half(core, value, None)
    total = place_half(1 - core, got, total)
    return (conv_out, feature_grad, total.reshape(KV, C, C))


def solution(mesh):
    in_specs = (
        P(AXES, None, None),
        P(AXES, None),
        P(AXES),
        P(),
        P(AXES, None, None),
    )
    out_specs = (P(AXES, None, None), P(AXES, None, None), P())
    return jax.shard_map(body, mesh=mesh, in_specs=in_specs, out_specs=out_specs, check_vma=False)
```
